32 devices in a mesh: tm: 4 (over x, core), rep: 8 (over z, y).
Axes of the slice: x: 2, y: 2, z: 4, core: 2. Of those that a mesh axis runs over, the one named last changes fastest.
Arguments:
- snapshots: float32 [32, 256, 1024], P('tm', 'rep'), may hold values from -6 to 6
- freq_bins: int32 [32], replicated, may hold values from 1 to 511
- replicas: float32 [2, 32, 8192, 256], P(None, 'tm', 'rep'), may hold values from -6 to 6
Outputs:
- power: float32 [8192], P(('rep', 'tm'))
The draws below stay inside these ranges and needn't reach their ends.
All inputs are finite; a program needn't handle non-finite values.
Results may differ from the reference program's by a relative error of at most 0.00005.
Values sent between devices are 32-bit elements; how exact they have to be, the bound alone decides.
No kernel may reach another device: no remote copies, remote signals or barrier semaphores. Data moves between devices by JAX's collectives and lax.ppermute only.
A program may use at most 64 MiB of HBM per device.

```python
import math
import jax
import jax.numpy as jnp
from jax import lax

ELEMS = 256
SAMPLES = 1024
BINS = 32
SNAPS = 32
GRID = 8192


def place_ends(drawn, own_key, low, high):
    extent = drawn.shape
    index_at = [jax.random.randint(jax.random.fold_in(own_key, axis), (), 0, extent[axis]) for axis in range(len(extent))]
    drawn = drawn.at[tuple(index_at)].set(low)
    longest = extent.index(max(extent))
    index_at[longest] = (index_at[longest] + 1) % extent[longest]
    return drawn.at[tuple(index_at)].set(high)


def block_levels(rng, shape, split, smallest, high):
    def one(dim, parts):
        draws = jax.random.uniform(jax.random.fold_in(jax.random.fold_in(rng, 6), dim), (parts,), jnp.float32, smallest / len(split), high / len(split))
        return jnp.repeat(jnp.exp(draws), shape[dim] // parts).reshape((-1,) + (1,) * (len(shape) - dim - 1))

    loudness = one(*split[0])
    for cut in split[1:]:
        loudness = loudness * one(*cut)
    return loudness


def normal_values(key, dims, scale, most, shards=(), kind=jnp.bfloat16):
    factor_of = block_levels(key, dims, shards, -0.22, 0.18) if shards else 1.0
    entries = jax.random.normal(key, dims, jnp.float32) * scale * factor_of
    return jnp.minimum(jnp.maximum(entries, -most), most).astype(kind)


def setup_inputs(seed: int = 0) -> dict:
    seeds = jax.random.split(jax.random.key(seed), 4)
    snapshots = normal_values(seeds[0], (SNAPS, ELEMS, SAMPLES), 1.0, 6.0, ((0, 4), (1, 8)), jnp.float32)
    freq_bins = place_ends(jax.random.randint(seeds[1], (BINS,), 1, SAMPLES // 2), jax.random.fold_in(seeds[1], 1), 1, (SAMPLES // 2) - 1).astype(jnp.int32)
    replicas = normal_values(seeds[2], (2, BINS, GRID, ELEMS), 1.0, 6.0, ((1, 4), (2, 8)), jnp.float32)
    return dict(snapshots=snapshots, freq_bins=freq_bins, replicas=replicas)


epsilon = 1e-6


def dft_table(freq_bins, length):
    offsets = jnp.arange(length, dtype=jnp.int32)
    phases = (offsets[:, None] * freq_bins[None, :]) % length
    angles = phases.astype(jnp.float32) * (2.0 * math.pi / length)
    window = 0.5 - 0.5 * jnp.cos(offsets.astype(jnp.float32) * (2.0 * math.pi / length))
    return jnp.concatenate([window[:, None] * jnp.cos(angles), -window[:, None] * jnp.sin(angles)], axis=1)


def reference(snapshots, freq_bins, replicas):
    dft_rows = dft_table(freq_bins, SAMPLES)
    spectra = jnp.dot(snapshots.reshape(SNAPS * ELEMS, SAMPLES), dft_rows, precision=lax.Precision.HIGHEST, preferred_element_type=jnp.float32).reshape(SNAPS, ELEMS, 2, BINS)

    def one_bin(column):
        spec_re = lax.dynamic_index_in_dim(spectra[:, :, 0, :], column, 2, keepdims=False)
        spec_im = lax.dynamic_index_in_dim(spectra[:, :, 1, :], column, 2, keepdims=False)
        rep_pair = lax.dynamic_index_in_dim(replicas, column, 1, keepdims=False)
        rep_re = rep_pair[0]
        rep_im = rep_pair[1]
        power_trace = jnp.sum(spec_re * spec_re + spec_im * spec_im) / SNAPS + epsilon
        norm_sq = jnp.sum(rep_re * rep_re + rep_im * rep_im, axis=1) + epsilon
        proj_re = jnp.dot(rep_re, spec_re.T, precision=lax.Precision.HIGHEST, preferred_element_type=jnp.float32) + jnp.dot(rep_im, spec_im.T, precision=lax.Precision.HIGHEST, preferred_element_type=jnp.float32)
        proj_im = jnp.dot(rep_re, spec_im.T, precision=lax.Precision.HIGHEST, preferred_element_type=jnp.float32) - jnp.dot(rep_im, spec_re.T, precision=lax.Precision.HIGHEST, preferred_element_type=jnp.float32)
        quadratic = jnp.sum(proj_re * proj_re + proj_im * proj_im, axis=1) / SNAPS
        return quadratic / (norm_sq * power_trace / ELEMS)

    per_bin = lax.map(one_bin, jnp.arange(BINS, dtype=jnp.int32))
    return jnp.sum(per_bin, axis=0) / BINS
```

```python
import functools
import math

import jax
import jax.numpy as jnp
from jax import lax
from jax.experimental import pallas as pl
from jax.experimental.pallas import tpu as pltpu
from jax.sharding import PartitionSpec as P

EPS = 1e-06
HIGHEST = lax.Precision.HIGHEST
F32 = jnp.float32
BF16 = jnp.bfloat16


def split(x):
    high = x.astype(BF16)
    return high, (x - high.astype(F32)).astype(BF16)


def dft_kernel(owners, repeats, bins_ref, snap_ref, out_ref, table_ref):
    snaps, elems, samples = snap_ref.shape
    bins = bins_ref.shape[0]
    cols = 2 * bins
    group = cols // owners
    fine = 2 ** (samples.bit_length() // 2)
    while samples % fine:
        fine //= 2
    coarse = samples // fine
    turn = 2.0 * math.pi / samples

    lane = lax.broadcasted_iota(jnp.int32, (1, cols), 1)
    bin_row = jnp.zeros((1, cols), jnp.int32)
    for k in range(bins):
        bin_row = jnp.where(lane // 2 == k, bins_ref[k], bin_row)
    odd = lane % 2 == 1

    def angle(count, step, freq):
        steps = lax.broadcasted_iota(jnp.int32, (count, cols), 0) * step
        return (steps * freq % samples).astype(F32) * turn

    angle_c, angle_f = angle(coarse, fine, bin_row), angle(fine, 1, bin_row)
    cos_c, sin_c = jnp.cos(angle_c), jnp.sin(angle_c)
    cos_f, sin_f = jnp.cos(angle_f), jnp.sin(angle_f)
    left = jnp.where(odd, -sin_c, cos_c)
    right = jnp.where(odd, cos_c, sin_c)
    win_c, win_f = angle(coarse, fine, 1), angle(fine, 1, 1)
    wcos_c, wsin_c = jnp.cos(win_c), jnp.sin(win_c)
    wcos_f, wsin_f = jnp.cos(win_f), jnp.sin(win_f)
    for a in range(coarse):
        row = slice(a, a + 1)
        window = 0.5 - 0.5 * (wcos_c[row] * wcos_f - wsin_c[row] * wsin_f)
        table_ref[a * fine : (a + 1) * fine, :] = window * (left[row] * cos_f - right[row] * sin_f)

    spectra = jnp.dot(
        snap_ref[...].reshape(snaps * elems, samples), table_ref[...], precision=HIGHEST, preferred_element_type=F32
    )
    width = snaps * group
    source = lax.broadcasted_iota(jnp.int32, (width, width), 0)
    target = lax.broadcasted_iota(jnp.int32, (width, width), 1)
    order = jnp.where(source == target % snaps * group + target // snaps, 1.0, 0.0)
    for t in range(owners):
        pieces = [spectra[s * elems : (s + 1) * elems, t * group : (t + 1) * group] for s in range(snaps)]
        message = jnp.dot(
            jnp.concatenate(pieces, axis=1), order, precision=HIGHEST, preferred_element_type=F32
        )
        for r in range(repeats):
            out_ref[r, t] = message


def main_kernel(total_snaps, bins, spec_ref, rep_ref, out_ref, sum_ref):
    reps, owners, elems, width = spec_ref.shape
    local_bins = pl.num_programs(0)
    col = pl.program_id(0)
    grid_rows, elem_count = rep_ref.shape[2], rep_ref.shape[3]
    chunk = out_ref.shape[1]

    @pl.when(col == 0)
    def _():
        sum_ref[...] = jnp.zeros_like(sum_ref)

    group = 2 * (total_snaps // owners)
    lanes = owners * group
    pieces = []
    for t in range(owners):
        block = spec_ref[:, t].reshape(reps * elems, width)
        rolled = pltpu.roll(block, width - col * group, 1) if width > group else block
        pieces.append(rolled[:, :group])
    spec = jnp.concatenate(pieces, axis=1)
    trace = jnp.sum(spec * spec) / total_snaps + EPS
    half = group // 2
    place = lax.broadcasted_iota(jnp.int32, spec.shape, 1) % group
    turned = jnp.where(place < half, pltpu.roll(spec, lanes - half, 1), -pltpu.roll(spec, half, 1))
    spec_hi, spec_lo = split(spec)
    turned_hi, turned_lo = split(turned)
    zero = jnp.zeros_like(spec_hi)
    right_re = jnp.concatenate([spec_hi, spec_lo], axis=1)
    right_im = jnp.concatenate([turned_hi, turned_lo], axis=1)
    low_re = jnp.concatenate([spec_hi, zero], axis=1)
    low_im = jnp.concatenate([turned_hi, zero], axis=1)
    dot = functools.partial(jnp.dot, preferred_element_type=F32)
    factor = 0.5 * elem_count / (trace * total_snaps * bins)
    tile = chunk
    for k in range(grid_rows // tile):
        rows = slice(k * tile, (k + 1) * tile)
        re, im = rep_ref[0, 0, rows], rep_ref[1, 0, rows]
        norm = jnp.sum(re * re + im * im, axis=1, keepdims=True) + EPS
        re_hi, re_lo = split(re)
        im_hi, im_lo = split(im)
        proj = dot(re_hi, right_re) + dot(im_hi, right_im) + dot(re_lo, low_re) + dot(im_lo, low_im)
        proj = proj + pltpu.roll(proj, lanes, 1)
        sum_ref[rows] += proj * proj * (factor / norm)

    @pl.when(col == local_bins - 1)
    def _():
        ones = jnp.ones((8, sum_ref.shape[1]), F32)
        for k in range(out_ref.shape[0]):
            block = sum_ref[k * chunk : (k + 1) * chunk]
            row = lax.dot_general(
                ones, block, (((1,), (1,)), ((), ())), precision=HIGHEST, preferred_element_type=F32
            )
            out_ref[k : k + 1] = row[0:1]


def partners(count, step):
    if count & (count - 1) == 0:
        return [(i, i ^ step) for i in range(count)]
    return [(i, (i + step) % count) for i in range(count)]


def shards(tm, rep, snapshots, freq_bins, replicas):
    snaps, elems, samples = snapshots.shape
    bins = freq_bins.shape[0]
    _, local_bins, grid_rows, elem_count = replicas.shape
    width = 2 * local_bins * snaps
    total_snaps = snaps * tm
    messages = pl.pallas_call(
        functools.partial(dft_kernel, tm, rep),
        out_shape=jax.ShapeDtypeStruct((rep, tm, elems, width), F32),
        in_specs=[pl.BlockSpec(memory_space=pltpu.SMEM), pl.BlockSpec(memory_space=pltpu.VMEM)],
        out_specs=pl.BlockSpec(memory_space=pltpu.VMEM),
        scratch_shapes=[pltpu.VMEM((samples, 2 * bins), F32)],
        compiler_params=pltpu.CompilerParams(vmem_limit_bytes=24 * 2**20),
        name="dft",
    )(freq_bins, snapshots)
    spectra = lax.all_to_all(
        messages.reshape(rep * tm, elems, width), ("rep", "tm"), split_axis=0, concat_axis=0, tiled=True
    ).reshape(rep, tm, elems, width)
    partial = pl.pallas_call(
        functools.partial(main_kernel, total_snaps, bins),
        grid=(local_bins,),
        out_shape=jax.ShapeDtypeStruct((tm, grid_rows // tm), F32),
        in_specs=[
            pl.BlockSpec((rep, tm, elems, width), lambda f: (0, 0, 0, 0)),
            pl.BlockSpec((2, 1, grid_rows, elem_count), lambda f: (0, f, 0, 0)),
        ],
        out_specs=pl.BlockSpec((tm, grid_rows // tm), lambda f: (0, 0)),
        scratch_shapes=[pltpu.VMEM((grid_rows, 4 * total_snaps), F32)],
        compiler_params=pltpu.CompilerParams(vmem_limit_bytes=32 * 2**20),
        name="power",
    )(spectra, replicas)
    me = lax.axis_index("tm")
    result = lax.dynamic_index_in_dim(partial, me, 0, keepdims=False)
    for step in range(1, tm):
        to = me ^ step if tm & (tm - 1) == 0 else (me + step) % tm
        mine = lax.dynamic_index_in_dim(partial, to, 0, keepdims=False)
        result = result + lax.ppermute(mine, "tm", partners(tm, step))
    return result


def solution(mesh):
    in_specs = (P("tm", "rep", None), P(), P(None, "tm", "rep", None))
    body = functools.partial(shards, mesh.shape["tm"], mesh.shape["rep"])
    return jax.shard_map(body, mesh=mesh, in_specs=in_specs, out_specs=P(("rep", "tm")), check_vma=False)
```

```python
import functools
import math

import jax
import jax.numpy as jnp
from jax import lax
from jax.experimental import pallas as pl
from jax.experimental.pallas import tpu as pltpu
from jax.sharding import PartitionSpec as P

EPS = 1e-06
HIGHEST = lax.Precision.HIGHEST
F32 = jnp.float32
BF16 = jnp.bfloat16
MIB = 2**20


def dot(left, right):
    return jnp.dot(left, right, preferred_element_type=F32)


def halves(x):
    high = x.astype(BF16).astype(F32)
    return high, x - high


def dft_kernel(owners, bins_hbm, snap_hbm, out_ref, snap_ref, bins_ref, table_ref, sems):
    snaps, elems, samples = snap_ref.shape
    bins = bins_ref.shape[0]
    load_bins = pltpu.make_async_copy(bins_hbm, bins_ref, sems.at[0])
    load_snaps = pltpu.make_async_copy(snap_hbm, snap_ref, sems.at[1])
    load_bins.start()
    load_snaps.start()
    me = lax.axis_index("tm")
    cols = 2 * bins
    group = cols // owners
    fine = 1
    while fine * fine < samples and samples % (2 * fine) == 0:
        fine *= 2
    coarse = samples // fine
    turn = 2.0 * math.pi / samples

    def angle(count, step, freq):
        steps = lax.broadcasted_iota(jnp.int32, (count, cols), 0) * step
        return (steps * freq % samples).astype(F32) * turn

    win_c, win_f = angle(coarse, fine, 1), angle(fine, 1, 1)
    wcos_c, wsin_c = jnp.cos(win_c), jnp.sin(win_c)
    wcos_f, wsin_f = jnp.cos(win_f), jnp.sin(win_f)
    lane = lax.broadcasted_iota(jnp.int32, (1, cols), 1)
    odd = lane % 2 == 1
    bin_row = jnp.zeros((1, cols), jnp.int32)
    load_bins.wait()
    for d in range(owners):
        for f in range(group // 2):
            value = bins_ref[(me ^ d) * (group // 2) + f]
            bin_row = jnp.where(lane // 2 == d * (group // 2) + f, value, bin_row)
    angle_c, angle_f = angle(coarse, fine, bin_row), angle(fine, 1, bin_row)
    cos_c, sin_c = jnp.cos(angle_c), jnp.sin(angle_c)
    cos_f, sin_f = jnp.cos(angle_f), jnp.sin(angle_f)
    left = jnp.where(odd, -sin_c, cos_c)
    right = jnp.where(odd, cos_c, sin_c)
    for a in range(coarse):
        row = slice(a, a + 1)
        window = 0.5 - 0.5 * (wcos_c[row] * wcos_f - wsin_c[row] * wsin_f)
        high, low = halves(window * (left[row] * cos_f - right[row] * sin_f))
        table_ref[a * fine : (a + 1) * fine, :] = jnp.concatenate([high, low], axis=1).astype(BF16)
    load_snaps.wait()
    high, low = halves(snap_ref[...].reshape(snaps * elems, samples))
    product = dot(high.astype(BF16), table_ref[...]) + dot(low.astype(BF16), table_ref[...])
    spectra = product[:, :cols] + product[:, cols:]

    width = snaps * group
    source = lax.broadcasted_iota(jnp.int32, (width, width), 0)
    target = lax.broadcasted_iota(jnp.int32, (width, width), 1)
    order = jnp.where(source == target % snaps * group + target // snaps, 1.0, 0.0).astype(BF16)
    messages = jnp.concatenate(
        [
            jnp.concatenate(
                [spectra[s * elems : (s + 1) * elems, d * group : (d + 1) * group] for s in range(snaps)], axis=1
            )
            for d in range(owners)
        ],
        axis=0,
    )
    high, rest = halves(messages)
    middle, low = halves(rest)
    moved = dot(high.astype(BF16), order) + dot(middle.astype(BF16), order) + dot(low.astype(BF16), order)
    out_ref[...] = moved.reshape(out_ref.shape)


def pack_kernel(local_bins, *refs):
    *blocks, out_ref = refs
    parts = [ref[k] for ref in blocks for k in range(ref.shape[0])]
    group = parts[0].shape[1] // local_bins
    out_ref[0] = jnp.concatenate(
        [part[:, f * group : (f + 1) * group] for f in range(local_bins) for part in parts], axis=1
    )


def prepare_kernel(elems, rep_ref, high_ref, low_ref):
    f = pl.program_id(0)
    rows, elem_count = rep_ref.shape[2:]
    tile = math.gcd(rows, 128)
    step = 128 if 128 % (2 * elems) == 0 and elem_count % 128 == 0 else elem_count
    lane = lax.broadcasted_iota(jnp.int32, (tile, step), 1)
    even = lane // elems % 2 == 0

    def body(k, _):
        at = pl.ds(pl.multiple_of(k * tile, tile), tile)
        re, im = rep_ref[0, 0, at], rep_ref[1, 0, at]
        scale = lax.rsqrt(jnp.sum(re * re + im * im, axis=1, keepdims=True) + EPS)
        for j in range(elem_count // step):
            cut = slice(j * step, (j + 1) * step)
            real, imag = re[:, cut] * scale, im[:, cut] * scale
            pair = (
                jnp.where(even, real, pltpu.roll(imag, elems, 1)),
                jnp.where(even, pltpu.roll(real, step - elems, 1), imag),
            )
            for a in range(2):
                high = pair[a].astype(BF16)
                high_ref[a, f, at, cut] = high
                low_ref[a, f, at, cut] = (pair[a] - high.astype(F32)).astype(BF16)
        return 0

    lax.fori_loop(0, rows // tile, body, 0)


def operand(spec_ref, f, lanes, half, side, me, bits):
    count = spec_ref.shape[0]
    blocks = []
    for p in range(count):
        apart = (2 * p + side) ^ me
        slot = 0
        for k in range(1, bits):
            slot = slot + ((apart >> k) & 1) * (1 << (bits - 1 - k))
        block = spec_ref[slot, :, f * lanes : (f + 1) * lanes]
        place = lax.broadcasted_iota(jnp.int32, block.shape, 1) % (2 * half)
        turned = jnp.where(place < half, pltpu.roll(block, lanes - half, 1), -pltpu.roll(block, half, 1))
        blocks += [block, turned]
    high, low = halves(jnp.concatenate(blocks, axis=0))
    return jnp.concatenate([high, low], axis=1).astype(BF16)


def first_kernel(half, bits, spec_ref, high_ref, low_ref, proj_ref):
    _, local_bins, rows, _ = high_ref.shape
    lanes = spec_ref.shape[2] // local_bins
    me = lax.axis_index("rep")
    side = me & 1
    for f in range(local_bins):
        right = operand(spec_ref, f, lanes, half, side, me, bits)
        proj_ref[f] = dot(high_ref[side, f], right) + dot(low_ref[side, f], right)


def second_kernel(bins, half, bits, spec_ref, own_ref, proj_ref, high_ref, low_ref, out_ref, sum_ref):
    _, local_bins, rows, elem_count = high_ref.shape
    lanes = spec_ref.shape[2] // local_bins
    total_snaps = lanes // 2
    chunk = out_ref.shape[1]
    me = lax.axis_index("rep")
    side = 1 - (me & 1)
    for f in range(local_bins):
        right = operand(spec_ref, f, lanes, half, side, me ^ 1, bits)
        cut = slice(f * lanes, (f + 1) * lanes)
        mine, other = own_ref[:, :, cut], spec_ref[:, :, cut]
        trace = jnp.sum(mine * mine + other * other) / total_snaps + EPS
        factor = 0.5 * elem_count / (trace * total_snaps * bins)
        for k in range(out_ref.shape[0]):
            at = slice(k * chunk, (k + 1) * chunk)
            proj = proj_ref[f, at] + dot(high_ref[side, f, at], right) + dot(low_ref[side, f, at], right)
            proj += pltpu.roll(proj, lanes, 1)
            value = proj * proj * factor
            sum_ref[at] = value if f == 0 else sum_ref[at] + value
    ones = jnp.ones((8, 2 * lanes), F32)
    for k in range(out_ref.shape[0]):
        block = sum_ref[k * chunk : (k + 1) * chunk]
        row = lax.dot_general(ones, block, (((1,), (1,)), ((), ())), precision=HIGHEST, preferred_element_type=F32)
        out_ref[k : k + 1] = row[0:1]


def swap(x, axis, count, bit):
    return lax.ppermute(x, axis, [(i, i ^ bit) for i in range(count)])


def bits_of(count):
    assert count & (count - 1) == 0
    return [1 << k for k in reversed(range(count.bit_length() - 1))]


def shards(tm, rep, snapshots, freq_bins, replicas):
    snaps, elems, samples = snapshots.shape
    bins = freq_bins.shape[0]
    _, local_bins, rows, elem_count = replicas.shape
    width = 2 * local_bins * snaps
    lanes = 2 * snaps * tm
    vmem = pl.BlockSpec(memory_space=pltpu.VMEM)
    hbm = pl.BlockSpec(memory_space=pltpu.HBM)
    parts = (2, local_bins, rows, elem_count)
    high, low = pl.pallas_call(
        functools.partial(prepare_kernel, elems),
        grid=(local_bins,),
        out_shape=(pltpu.VMEM(parts, BF16), pltpu.VMEM(parts, BF16)),
        in_specs=[pl.BlockSpec((2, 1, rows, elem_count), lambda f: (0, f, 0, 0))],
        out_specs=[vmem] * 2,
        compiler_params=pltpu.CompilerParams(vmem_limit_bytes=32 * MIB),
        cost_estimate=pl.CostEstimate(flops=8 * replicas.size, bytes_accessed=4 * replicas.size, transcendentals=0),
        name="prepare",
    )(replicas)
    messages = pl.pallas_call(
        functools.partial(dft_kernel, tm),
        out_shape=jax.ShapeDtypeStruct((tm, elems, width), F32),
        in_specs=[hbm, hbm],
        out_specs=vmem,
        scratch_shapes=[
            pltpu.VMEM(snapshots.shape, F32),
            pltpu.SMEM((bins,), jnp.int32),
            pltpu.VMEM((samples, 4 * bins), BF16),
            pltpu.SemaphoreType.DMA((2,)),
        ],
        compiler_params=pltpu.CompilerParams(vmem_limit_bytes=48 * MIB),
        name="dft",
    )(freq_bins, snapshots)
    held = [messages]
    for bit in bits_of(tm):
        away = jnp.concatenate([h[bit:] for h in held]) if len(held) > 1 else held[0][bit:]
        came = swap(away, "tm", tm, bit)
        held = [h[:bit] for h in held] + [came[k * bit : (k + 1) * bit] for k in range(len(held))]
    spectra = pl.pallas_call(
        functools.partial(pack_kernel, local_bins),
        out_shape=jax.ShapeDtypeStruct((1, elems, local_bins * lanes), F32),
        in_specs=[vmem] * len(held),
        out_specs=vmem,
        compiler_params=pltpu.CompilerParams(vmem_limit_bytes=4 * MIB),
        name="pack",
    )(*held)
    *early, last = bits_of(rep)
    for bit in early:
        spectra = jnp.concatenate([spectra, swap(spectra, "rep", rep, bit)])
    other = swap(spectra, "rep", rep, last)
    bits = rep.bit_length() - 1
    work = 2 * rows * elem_count * lanes * local_bins * 2
    proj = pl.pallas_call(
        functools.partial(first_kernel, snaps, bits),
        out_shape=pltpu.VMEM((local_bins, rows, 2 * lanes), F32),
        in_specs=[vmem] * 3,
        out_specs=vmem,
        compiler_params=pltpu.CompilerParams(vmem_limit_bytes=12 * MIB),
        cost_estimate=pl.CostEstimate(flops=work, bytes_accessed=2 * replicas.size, transcendentals=0),
        name="first",
    )(spectra, high, low)
    partial = pl.pallas_call(
        functools.partial(second_kernel, bins, snaps, bits),
        out_shape=jax.ShapeDtypeStruct((tm, rows // tm), F32),
        in_specs=[vmem] * 5,
        out_specs=vmem,
        scratch_shapes=[pltpu.VMEM((rows, 2 * lanes), F32)],
        compiler_params=pltpu.CompilerParams(vmem_limit_bytes=12 * MIB),
        name="second",
    )(other, spectra, proj, high, low)
    me = lax.axis_index("tm")
    result = lax.dynamic_index_in_dim(partial, me, 0, keepdims=False)
    for step in range(1, tm):
        mine = lax.dynamic_index_in_dim(partial, me ^ step, 0, keepdims=False)
        result = result + swap(mine, "tm", tm, step)
    return result


def solution(mesh):
    in_specs = (P("tm", "rep", None), P(), P(None, "tm", "rep", None))
    body = functools.partial(shards, mesh.shape["tm"], mesh.shape["rep"])
    return jax.shard_map(body, mesh=mesh, in_specs=in_specs, out_specs=P(("rep", "tm")), check_vma=False)
```

```python
import functools
import math

import jax
import jax.numpy as jnp
from jax import lax
from jax.experimental import pallas as pl
from jax.experimental.pallas import tpu as pltpu
from jax.sharding import PartitionSpec as P

EPS = 1e-06
HIGHEST = lax.Precision.HIGHEST
F32 = jnp.float32
BF16 = jnp.bfloat16
MIB = 2**20
COST = 2 * 10**10


def dot(left, right):
    return jnp.dot(left, right, preferred_element_type=F32)


def halves(x):
    high = x.astype(BF16).astype(F32)
    return high, x - high


def dft_kernel(owners, bins_hbm, snap_hbm, keep_ref, away_ref, snap_ref, bins_ref, table_ref, sems):
    snaps, elems, samples = snap_ref.shape
    bins = bins_ref.shape[0]
    load_bins = pltpu.make_async_copy(bins_hbm, bins_ref, sems.at[0])
    load_snaps = pltpu.make_async_copy(snap_hbm, snap_ref, sems.at[1])
    load_bins.start()
    load_snaps.start()
    me = lax.axis_index("tm")
    cols = 2 * bins
    group = cols // owners
    fine = 1
    while fine * fine < samples and samples % (2 * fine) == 0:
        fine *= 2
    coarse = samples // fine
    turn = 2.0 * math.pi / samples

    def angle(count, step, freq):
        steps = lax.broadcasted_iota(jnp.int32, (count, cols), 0) * step
        return (steps * freq % samples).astype(F32) * turn

    win_c, win_f = angle(coarse, fine, 1), angle(fine, 1, 1)
    wcos_c, wsin_c = jnp.cos(win_c), jnp.sin(win_c)
    wcos_f, wsin_f = jnp.cos(win_f), jnp.sin(win_f)
    lane = lax.broadcasted_iota(jnp.int32, (1, cols), 1)
    odd = lane % 2 == 1
    bin_row = jnp.zeros((1, cols), jnp.int32)
    load_bins.wait()
    for d in range(owners):
        for f in range(group // 2):
            value = bins_ref[(me ^ d) * (group // 2) + f]
            bin_row = jnp.where(lane // 2 == d * (group // 2) + f, value, bin_row)
    angle_c, angle_f = angle(coarse, fine, bin_row), angle(fine, 1, bin_row)
    cos_c, sin_c = jnp.cos(angle_c), jnp.sin(angle_c)
    cos_f, sin_f = jnp.cos(angle_f), jnp.sin(angle_f)
    left = jnp.where(odd, -sin_c, cos_c)
    right = jnp.where(odd, cos_c, sin_c)
    for a in range(coarse):
        row = slice(a, a + 1)
        window = 0.5 - 0.5 * (wcos_c[row] * wcos_f - wsin_c[row] * wsin_f)
        high, low = halves(window * (left[row] * cos_f - right[row] * sin_f))
        table_ref[a * fine : (a + 1) * fine, :] = jnp.concatenate([high, low], axis=1).astype(BF16)
    load_snaps.wait()
    high, low = halves(snap_ref[...].reshape(snaps * elems, samples))
    product = dot(high.astype(BF16), table_ref[...]) + dot(low.astype(BF16), table_ref[...])
    spectra = product[:, :cols] + product[:, cols:]

    width = snaps * group
    source = lax.broadcasted_iota(jnp.int32, (width, width), 0)
    target = lax.broadcasted_iota(jnp.int32, (width, width), 1)
    order = jnp.where(source == target % snaps * group + target // snaps, 1.0, 0.0).astype(BF16)
    messages = jnp.concatenate(
        [
            jnp.concatenate(
                [spectra[s * elems : (s + 1) * elems, d * group : (d + 1) * group] for s in range(snaps)], axis=1
            )
            for d in range(owners)
        ],
        axis=0,
    )
    high, rest = halves(messages)
    middle, low = halves(rest)
    moved = dot(high.astype(BF16), order) + dot(middle.astype(BF16), order) + dot(low.astype(BF16), order)
    moved = moved.reshape((owners,) + keep_ref.shape[1:])
    keep_ref[...] = moved[: keep_ref.shape[0]]
    away_ref[...] = moved[keep_ref.shape[0] :]


def pack_kernel(local_bins, slots, *refs):
    *blocks, out_ref = refs
    for n in range(out_ref.shape[0]):
        parts = [blocks[k][b] for k, b in slots[n]]
        group = parts[0].shape[1] // local_bins
        out_ref[n] = jnp.concatenate(
            [part[:, f * group : (f + 1) * group] for f in range(local_bins) for part in parts], axis=1
        )


def collect_kernel(after_ref, *refs):
    del after_ref
    *blocks, out_ref = refs
    for k, block in enumerate(blocks):
        out_ref[k] = block[1]


def prepare_kernel(first, elems, after_ref, rep_hbm, high_ref, low_ref, rep_ref, scale_ref, sems):
    del after_ref
    rows, elem_count = rep_ref.shape[2:]
    tile = math.gcd(rows, 256)
    step = 128 if 128 % (2 * elems) == 0 and elem_count % 128 == 0 else elem_count
    lane = lax.broadcasted_iota(jnp.int32, (tile, step), 1)
    even = lane // elems % 2 == 0
    ones = jnp.ones((elem_count, 128), BF16)
    count = high_ref.shape[1]
    loads = [
        [pltpu.make_async_copy(rep_hbm.at[part, first + i], rep_ref.at[part, i], sems.at[part, i]) for part in range(2)]
        for i in range(count)
    ]
    for pair in loads:
        for load in pair:
            load.start()
    for i in range(count):
        for load in loads[i]:
            load.wait()
        re, im = rep_ref[0, i], rep_ref[1, i]
        high, low = halves(re * re + im * im)
        norm = dot(high.astype(BF16), ones) + dot(low.astype(BF16), ones) + EPS
        scale_ref[i] = lax.rsqrt(norm)
        for k in range(rows // tile):
            at = slice(k * tile, (k + 1) * tile)
            scale = scale_ref[i, at]
            for j in range(elem_count // step):
                cut = slice(j * step, (j + 1) * step)
                wide = jnp.concatenate([scale] * (step // 128), axis=1)
                real, imag = rep_ref[0, i, at, cut] * wide, rep_ref[1, i, at, cut] * wide
                pair = (
                    jnp.where(even, real, pltpu.roll(imag, elems, 1)),
                    jnp.where(even, pltpu.roll(real, step - elems, 1), imag),
                )
                for a in range(2):
                    high = pair[a].astype(BF16)
                    high_ref[a, i, at, cut] = high
                    low_ref[a, i, at, cut] = (pair[a] - high.astype(F32)).astype(BF16)


def operand(spec_ref, f, lanes, half, side, me, bits):
    count = spec_ref.shape[0]
    blocks = []
    for p in range(count):
        apart = (2 * p + side) ^ me
        slot = 0
        for k in range(1, bits):
            slot = slot + ((apart >> k) & 1) * (1 << (bits - 1 - k))
        block = spec_ref[slot, :, f * lanes : (f + 1) * lanes]
        place = lax.broadcasted_iota(jnp.int32, block.shape, 1) % (2 * half)
        turned = jnp.where(place < half, pltpu.roll(block, lanes - half, 1), -pltpu.roll(block, half, 1))
        blocks += [block, turned]
    high, low = halves(jnp.concatenate(blocks, axis=0))
    return jnp.concatenate([high, low], axis=1).astype(BF16)


def first_kernel(half, bits, spec_ref, *refs):
    *parts, proj_ref = refs
    local_bins = proj_ref.shape[0]
    each = parts[0].shape[1]
    lanes = spec_ref.shape[2] // local_bins
    me = lax.axis_index("rep")
    side = me & 1
    for f in range(local_bins):
        right = operand(spec_ref, f, lanes, half, side, me, bits)
        high_ref, low_ref = parts[f // each * 2 : f // each * 2 + 2]
        proj_ref[f] = dot(high_ref[side, f % each], right) + dot(low_ref[side, f % each], right)


def second_kernel(elem_count, bins, half, bits, count, spec_ref, own_ref, proj_ref, *refs):
    *refs, row_ref, sum_ref = refs
    parts, outs = refs[:count], refs[count:]
    local_bins = proj_ref.shape[0]
    each = parts[0].shape[1]
    lanes = spec_ref.shape[2] // local_bins
    total_snaps = lanes // 2
    chunk = row_ref.shape[2]
    me = lax.axis_index("rep")
    side = 1 - (me & 1)
    for f in range(local_bins):
        high_ref, low_ref = parts[f // each * 2 : f // each * 2 + 2]
        right = operand(spec_ref, f, lanes, half, side, me ^ 1, bits)
        cut = slice(f * lanes, (f + 1) * lanes)
        mine, other = own_ref[:, :, cut], spec_ref[:, :, cut]
        trace = jnp.sum(mine * mine + other * other) / total_snaps + EPS
        factor = 0.5 * elem_count / (trace * total_snaps * bins)
        for k in range(row_ref.shape[0]):
            at = slice(k * chunk, (k + 1) * chunk)
            proj = proj_ref[f, at] + dot(high_ref[side, f % each, at], right)
            proj += dot(low_ref[side, f % each, at], right)
            proj += pltpu.roll(proj, lanes, 1)
            value = proj * proj * factor
            sum_ref[at] = value if f == 0 else sum_ref[at] + value
    ones = jnp.ones((8, 2 * lanes), F32)
    for k in range(row_ref.shape[0]):
        block = sum_ref[k * chunk : (k + 1) * chunk]
        row = lax.dot_general(ones, block, (((1,), (1,)), ((), ())), precision=HIGHEST, preferred_element_type=F32)
        row_ref[k] = row[0:1]
    owner = lax.axis_index("tm")
    for d, out_ref in enumerate(outs):
        out_ref[...] = row_ref[owner ^ d]


def swap(x, mesh_shape, tm_bit, rep_bit):
    tm, rep = mesh_shape
    pairs = [(t * rep + r, (t ^ tm_bit) * rep + (r ^ rep_bit)) for t in range(tm) for r in range(rep)]
    return lax.ppermute(x, ("tm", "rep"), pairs)


def bits_of(count):
    assert count & (count - 1) == 0
    return [1 << k for k in reversed(range(count.bit_length() - 1))]


def shards(tm, rep, snapshots, freq_bins, replicas):
    snaps, elems, samples = snapshots.shape
    bins = freq_bins.shape[0]
    _, local_bins, rows, elem_count = replicas.shape
    width = 2 * local_bins * snaps
    lanes = 2 * snaps * tm
    vmem = pl.BlockSpec(memory_space=pltpu.VMEM)
    hbm = pl.BlockSpec(memory_space=pltpu.HBM)
    shape = (tm // 2, elems, width)
    keep, away = pl.pallas_call(
        functools.partial(dft_kernel, tm),
        out_shape=(pltpu.VMEM(shape, F32), pltpu.VMEM(shape, F32)),
        in_specs=[hbm, hbm],
        out_specs=[vmem] * 2,
        scratch_shapes=[
            pltpu.VMEM(snapshots.shape, F32),
            pltpu.SMEM((bins,), jnp.int32),
            pltpu.VMEM((samples, 4 * bins), BF16),
            pltpu.SemaphoreType.DMA((2,)),
        ],
        compiler_params=pltpu.CompilerParams(vmem_limit_bytes=60 * MIB),
        name="dft",
    )(freq_bins, snapshots)
    each = -(-local_bins // 2)

    def prepare(k, after):
        shape = (2, each, rows, elem_count)
        return pl.pallas_call(
            functools.partial(prepare_kernel, k * each, elems),
            out_shape=(pltpu.VMEM(shape, BF16), pltpu.VMEM(shape, BF16)),
            in_specs=[hbm, hbm],
            out_specs=[vmem] * 2,
            scratch_shapes=[
                pltpu.VMEM(shape, F32),
                pltpu.VMEM((each, rows, 128), F32),
                pltpu.SemaphoreType.DMA((2, each)),
            ],
            compiler_params=pltpu.CompilerParams(vmem_limit_bytes=36 * MIB),
            cost_estimate=pl.CostEstimate(flops=COST, bytes_accessed=0, transcendentals=0),
            name="prepare",
        )(after, replicas)

    send = functools.partial(swap, mesh_shape=(tm, rep))
    held = [(keep, away)]
    parts = prepare(0, keep)
    for bit in bits_of(tm)[:-2]:
        came = [send(b, tm_bit=bit, rep_bit=0) for _, b in held]
        kept = [a for a, _ in held] + came
        held = [(k[: bit // 2], k[bit // 2 :]) for k in kept]
    top, *middle = bits_of(rep)[:-2]
    near = [a for a, _ in held] + [send(b, tm_bit=2, rep_bit=0) for _, b in held]
    far = [send(a, tm_bit=0, rep_bit=top) for a, _ in held] + [send(b, tm_bit=2, rep_bit=top) for _, b in held]
    count = len(near)
    crossing = pl.pallas_call(
        collect_kernel,
        out_shape=pltpu.VMEM((2 * count, elems, width), F32),
        in_specs=[pl.BlockSpec(memory_space=pl.ANY)] + [vmem] * (2 * count),
        out_specs=vmem,
        compiler_params=pltpu.CompilerParams(vmem_limit_bytes=4 * MIB),
        name="collect",
    )(parts[1], *near, *far)
    came = send(crossing, tm_bit=1, rep_bit=0)
    slots = [[(n * count + k, 0) for k in range(count)] + [(2 * count, n * count + k) for k in range(count)] for n in range(2)]
    spectra = pl.pallas_call(
        functools.partial(pack_kernel, local_bins, slots),
        out_shape=pltpu.VMEM((2, elems, local_bins * lanes), F32),
        in_specs=[vmem] * (2 * count + 1),
        out_specs=vmem,
        compiler_params=pltpu.CompilerParams(vmem_limit_bytes=4 * MIB),
        name="pack",
    )(*near, *far, came)
    if each < local_bins:
        parts += prepare(1, spectra)
    for bit in middle:
        spectra = jnp.concatenate([spectra, send(spectra, tm_bit=0, rep_bit=bit)])
    own = jnp.concatenate([spectra, send(spectra, tm_bit=0, rep_bit=2)])
    other = jnp.concatenate([send(spectra, tm_bit=0, rep_bit=1), send(spectra, tm_bit=0, rep_bit=3)])
    bits = rep.bit_length() - 1
    proj = pl.pallas_call(
        functools.partial(first_kernel, snaps, bits),
        out_shape=pltpu.VMEM((local_bins, rows, 2 * lanes), F32),
        in_specs=[vmem] * (1 + len(parts)),
        out_specs=vmem,
        compiler_params=pltpu.CompilerParams(vmem_limit_bytes=6 * MIB),
        cost_estimate=pl.CostEstimate(flops=COST, bytes_accessed=0, transcendentals=0),
        name="first",
    )(own, *parts)
    chunk = rows // tm
    shares = pl.pallas_call(
        functools.partial(second_kernel, elem_count, bins, snaps, bits, len(parts)),
        out_shape=[pltpu.VMEM((1, chunk), F32)] * tm,
        in_specs=[vmem] * (3 + len(parts)),
        out_specs=[vmem] * tm,
        scratch_shapes=[pltpu.VMEM((tm, 1, chunk), F32), pltpu.VMEM((rows, 2 * lanes), F32)],
        compiler_params=pltpu.CompilerParams(vmem_limit_bytes=6 * MIB),
        name="second",
    )(other, own, proj, *parts)
    result = shares[0]
    for step in range(1, tm):
        result = result + send(shares[step], tm_bit=step, rep_bit=0)
    return result.reshape(chunk)


def solution(mesh):
    in_specs = (P("tm", "rep", None), P(), P(None, "tm", "rep", None))
    body = functools.partial(shards, mesh.shape["tm"], mesh.shape["rep"])
    return jax.shard_map(body, mesh=mesh, in_specs=in_specs, out_specs=P(("rep", "tm")), check_vma=False)
```

```python
import functools
import math

import jax
import jax.numpy as jnp
from jax import lax
from jax.experimental import pallas as pl
from jax.experimental.pallas import tpu as pltpu
from jax.sharding import PartitionSpec as P

EPS = 1e-06
F32 = jnp.float32
BF16 = jnp.bfloat16
MIB = 2**20
COST = 2 * 10**10


def dot(left, right):
    return jnp.dot(left, right, preferred_element_type=F32)


def halves(x):
    high = x.astype(BF16).astype(F32)
    return high, x - high


def dft_kernel(owners, bins_hbm, snap_hbm, keep_ref, away_ref, snap_ref, bins_ref, table_ref, sems):
    snaps, elems, samples = snap_ref.shape
    bins = bins_ref.shape[0]
    load_bins = pltpu.make_async_copy(bins_hbm, bins_ref, sems.at[0])
    load_snaps = pltpu.make_async_copy(snap_hbm, snap_ref, sems.at[1])
    load_bins.start()
    load_snaps.start()
    me = lax.axis_index("tm")
    cols = 2 * bins
    group = cols // owners
    fine = 1
    while fine * fine < samples and samples % (2 * fine) == 0:
        fine *= 2
    coarse = samples // fine
    turn = 2.0 * math.pi / samples

    def angle(count, step, freq):
        steps = lax.broadcasted_iota(jnp.int32, (count, cols), 0) * step
        return (steps * freq % samples).astype(F32) * turn

    win_c, win_f = angle(coarse, fine, 1), angle(fine, 1, 1)
    wcos_c, wsin_c = jnp.cos(win_c), jnp.sin(win_c)
    wcos_f, wsin_f = jnp.cos(win_f), jnp.sin(win_f)
    lane = lax.broadcasted_iota(jnp.int32, (1, cols), 1)
    odd = lane % 2 == 1
    bin_row = jnp.zeros((1, cols), jnp.int32)
    load_bins.wait()
    for d in range(owners):
        for f in range(group // 2):
            value = bins_ref[(me ^ d) * (group // 2) + f]
            bin_row = jnp.where(lane // 2 == d * (group // 2) + f, value, bin_row)
    angle_c, angle_f = angle(coarse, fine, bin_row), angle(fine, 1, bin_row)
    cos_c, sin_c = jnp.cos(angle_c), jnp.sin(angle_c)
    cos_f, sin_f = jnp.cos(angle_f), jnp.sin(angle_f)
    left = jnp.where(odd, -sin_c, cos_c)
    right = jnp.where(odd, cos_c, sin_c)
    for a in range(coarse):
        row = slice(a, a + 1)
        window = 0.5 - 0.5 * (wcos_c[row] * wcos_f - wsin_c[row] * wsin_f)
        high, low = halves(window * (left[row] * cos_f - right[row] * sin_f))
        table_ref[a * fine : (a + 1) * fine, :] = jnp.concatenate([high, low], axis=1).astype(BF16)
    load_snaps.wait()
    high, low = halves(snap_ref[...].reshape(snaps * elems, samples))
    product = dot(high.astype(BF16), table_ref[...]) + dot(low.astype(BF16), table_ref[...])
    spectra = product[:, :cols] + product[:, cols:]

    width = snaps * group
    source = lax.broadcasted_iota(jnp.int32, (width, width), 0)
    target = lax.broadcasted_iota(jnp.int32, (width, width), 1)
    order = jnp.where(source == target % snaps * group + target // snaps, 1.0, 0.0).astype(BF16)
    messages = jnp.concatenate(
        [
            jnp.concatenate(
                [spectra[s * elems : (s + 1) * elems, d * group : (d + 1) * group] for s in range(snaps)], axis=1
            )
            for d in range(owners)
        ],
        axis=0,
    )
    high, rest = halves(messages)
    middle, low = halves(rest)
    moved = dot(high.astype(BF16), order) + dot(middle.astype(BF16), order) + dot(low.astype(BF16), order)
    moved = moved.reshape((owners,) + keep_ref.shape[1:])
    keep_ref[...] = moved[: keep_ref.shape[0]]
    away_ref[...] = moved[keep_ref.shape[0] :]


def pack_kernel(local_bins, slots, *refs):
    *blocks, out_ref = refs
    for n in range(out_ref.shape[0]):
        parts = [blocks[k][b] for k, b in slots[n]]
        group = parts[0].shape[1] // local_bins
        out_ref[n] = jnp.concatenate(
            [part[:, f * group : (f + 1) * group] for f in range(local_bins) for part in parts], axis=1
        )


def collect_kernel(after_ref, *refs):
    del after_ref
    *blocks, out_ref = refs
    for k, block in enumerate(blocks):
        out_ref[k] = block[1]


def prepare_kernel(first, elems, after_ref, rep_hbm, high_ref, low_ref, inverse_ref, rep_ref, sems):
    del after_ref
    rows, elem_count = rep_ref.shape[2:]
    pieces = sems.shape[2]
    tile = rows // pieces
    step = 128 if 128 % (2 * elems) == 0 and elem_count % 128 == 0 else elem_count
    lane = lax.broadcasted_iota(jnp.int32, (tile, step), 1)
    even = lane // elems % 2 == 0
    ones = jnp.ones((elem_count, inverse_ref.shape[2]), BF16)
    bins = range(high_ref.shape[1])

    def load(part, i, k):
        at = slice(k * tile, (k + 1) * tile)
        return pltpu.make_async_copy(rep_hbm.at[part, first + i, at], rep_ref.at[part, i, at], sems.at[part, i, k])

    for i in bins:
        for k in range(pieces):
            for part in range(2):
                load(part, i, k).start()
    for i in bins:
        for k in range(pieces):
            for part in range(2):
                load(part, i, k).wait()
            at = slice(k * tile, (k + 1) * tile)
            re, im = rep_ref[0, i, at], rep_ref[1, i, at]
            high, low = halves(re * re + im * im)
            inverse_ref[i, at] = 1.0 / (dot(high.astype(BF16), ones) + dot(low.astype(BF16), ones) + EPS)
            for j in range(elem_count // step):
                cut = slice(j * step, (j + 1) * step)
                real, imag = rep_ref[0, i, at, cut], rep_ref[1, i, at, cut]
                pair = (
                    jnp.where(even, real, pltpu.roll(imag, elems, 1)),
                    jnp.where(even, pltpu.roll(real, step - elems, 1), imag),
                )
                for a in range(2):
                    high = pair[a].astype(BF16)
                    high_ref[a, i, at, cut] = high
                    low_ref[a, i, at, cut] = (pair[a] - high.astype(F32)).astype(BF16)


def operands(spec_ref, local_bins, half, side, me, bits):
    count = spec_ref.shape[0]
    lanes = spec_ref.shape[2] // local_bins
    paired = 2 * lanes == 128 and local_bins % 2 == 0
    span = 2 * lanes if paired else lanes
    slots = []
    for p in range(count):
        apart = (2 * p + side) ^ me
        slots.append(sum(((apart >> k) & 1) * (1 << (bits - 1 - k)) for k in range(1, bits)))
    result = []
    for q in range(spec_ref.shape[2] // span):
        blocks = []
        for slot in slots:
            block = spec_ref[slot, :, q * span : (q + 1) * span]
            place = lax.broadcasted_iota(jnp.int32, block.shape, 1) % (2 * half)
            turned = jnp.where(place < half, pltpu.roll(block, span - half, 1), -pltpu.roll(block, half, 1))
            blocks += [block, turned]
        high, low = halves(jnp.concatenate(blocks, axis=0))
        if paired:
            near = lax.broadcasted_iota(jnp.int32, high.shape, 1) < lanes
            result.append(jnp.where(near, high, pltpu.roll(low, lanes, 1)).astype(BF16))
            result.append(jnp.where(near, pltpu.roll(high, lanes, 1), low).astype(BF16))
        else:
            result.append(jnp.concatenate([high, low], axis=1).astype(BF16))
    return result


def first_kernel(half, bits, spec_ref, *refs):
    *parts, proj_ref = refs
    each = parts[0].shape[1]
    me = lax.axis_index("rep")
    side = me & 1
    for f, right in enumerate(operands(spec_ref, proj_ref.shape[0], half, side, me, bits)):
        high_ref, low_ref = parts[f // each * 2 : f // each * 2 + 2]
        proj_ref[f] = dot(high_ref[side, f % each], right) + dot(low_ref[side, f % each], right)


def rows_power(own_half, proj_ref, rights, factors, parts, inverses, out_ref, row_ref, sum_ref):
    count, chunk = row_ref.shape[0], row_ref.shape[2]
    each = parts[0].shape[1]
    lanes = proj_ref.shape[2] // 2
    side = 1 - (lax.axis_index("rep") & 1)
    owner = lax.axis_index("tm")
    top = owner // count if own_half else 1 - owner // count
    at = pl.ds(pl.multiple_of(top * count * chunk, count * chunk), count * chunk)
    for f in range(proj_ref.shape[0]):
        high_ref, low_ref = parts[f // each * 2 : f // each * 2 + 2]
        proj = proj_ref[f, at] + dot(high_ref[side, f % each, at], rights[f])
        proj += dot(low_ref[side, f % each, at], rights[f])
        proj += pltpu.roll(proj, lanes, 1)
        value = proj * proj * (inverses[f // each][f % each, at] * factors[f])
        sum_ref[...] = value if f == 0 else sum_ref[...] + value
    for k in range(count):
        row_ref[k] = jnp.sum(sum_ref[k * chunk : (k + 1) * chunk].T, axis=0, keepdims=True)
    for d in range(count):
        out_ref[d : d + 1] = row_ref[(owner ^ d) % count]


def second_kernel(elem_count, bins, half, bits, count, spec_ref, own_ref, proj_ref, *refs):
    parts, inverses = refs[: 2 * count], refs[2 * count : 3 * count]
    out_ref, right_ref, factor_ref, row_ref, sum_ref = refs[3 * count :]
    local_bins = proj_ref.shape[0]
    lanes = proj_ref.shape[2] // 2
    total_snaps = lanes // 2
    me = lax.axis_index("rep")
    rights = operands(spec_ref, local_bins, half, 1 - (me & 1), me ^ 1, bits)
    squares = 0.0
    for n in range(own_ref.shape[0]):
        mine, other = own_ref[n], spec_ref[n]
        squares = squares + (mine * mine + other * other)
    squares = jnp.sum(squares, axis=0, keepdims=True)
    factors = []
    for f in range(local_bins):
        trace = jnp.sum(squares[:, f * lanes : (f + 1) * lanes], axis=1, keepdims=True) / total_snaps + EPS
        factors.append(jnp.broadcast_to(0.5 * elem_count / (trace * total_snaps * bins), factor_ref.shape[1:]))
        factor_ref[f] = factors[f]
        right_ref[f] = rights[f]
    rows_power(False, proj_ref, rights, factors, parts, inverses, out_ref, row_ref, sum_ref)


def third_kernel(count, right_ref, factor_ref, proj_ref, *refs):
    parts, inverses, (out_ref, row_ref, sum_ref) = refs[: 2 * count], refs[2 * count : 3 * count], refs[3 * count :]
    rows_power(True, proj_ref, right_ref, factor_ref, parts, inverses, out_ref, row_ref, sum_ref)


def swap(x, mesh_shape, tm_bit, rep_bit):
    tm, rep = mesh_shape
    pairs = [(t * rep + r, (t ^ tm_bit) * rep + (r ^ rep_bit)) for t in range(tm) for r in range(rep)]
    return lax.ppermute(x, ("tm", "rep"), pairs)


def bits_of(count):
    assert count & (count - 1) == 0
    return [1 << k for k in reversed(range(count.bit_length() - 1))]


def shards(tm, rep, snapshots, freq_bins, replicas):
    snaps, elems, samples = snapshots.shape
    bins = freq_bins.shape[0]
    _, local_bins, rows, elem_count = replicas.shape
    width = 2 * local_bins * snaps
    lanes = 2 * snaps * tm
    vmem = pl.BlockSpec(memory_space=pltpu.VMEM)
    hbm = pl.BlockSpec(memory_space=pltpu.HBM)
    shape = (tm // 2, elems, width)
    keep, away = pl.pallas_call(
        functools.partial(dft_kernel, tm),
        out_shape=(pltpu.VMEM(shape, F32), pltpu.VMEM(shape, F32)),
        in_specs=[hbm, hbm],
        out_specs=[vmem] * 2,
        scratch_shapes=[
            pltpu.VMEM(snapshots.shape, F32),
            pltpu.SMEM((bins,), jnp.int32),
            pltpu.VMEM((samples, 4 * bins), BF16),
            pltpu.SemaphoreType.DMA((2,)),
        ],
        compiler_params=pltpu.CompilerParams(vmem_limit_bytes=60 * MIB),
        name="dft",
    )(freq_bins, snapshots)
    each = -(-local_bins // 2)

    def prepare(k, after):
        shape = (2, each, rows, elem_count)
        return pl.pallas_call(
            functools.partial(prepare_kernel, k * each, elems),
            out_shape=[pltpu.VMEM(shape, BF16), pltpu.VMEM(shape, BF16), pltpu.VMEM((each, rows, 2 * lanes), F32)],
            in_specs=[pl.BlockSpec(memory_space=pl.ANY), hbm],
            out_specs=[vmem] * 3,
            scratch_shapes=[
                pltpu.VMEM(shape, F32),
                pltpu.SemaphoreType.DMA((2, each, rows // math.gcd(rows, 512))),
            ],
            compiler_params=pltpu.CompilerParams(vmem_limit_bytes=34 * MIB),
            cost_estimate=pl.CostEstimate(flops=COST, bytes_accessed=0, transcendentals=0),
            name="prepare",
        )(after, replicas)

    send = functools.partial(swap, mesh_shape=(tm, rep))
    held = [(keep, away)]
    *parts, inverse = prepare(0, keep)
    inverses = [inverse]
    for bit in bits_of(tm)[:-2]:
        came = [send(b, tm_bit=bit, rep_bit=0) for _, b in held]
        kept = [a for a, _ in held] + came
        held = [(k[: bit // 2], k[bit // 2 :]) for k in kept]
    top, *middle = bits_of(rep)[:-2]
    near = [a for a, _ in held] + [send(b, tm_bit=2, rep_bit=0) for _, b in held]
    far = [send(a, tm_bit=0, rep_bit=top) for a, _ in held] + [send(b, tm_bit=2, rep_bit=top) for _, b in held]
    count = len(near)
    crossing = pl.pallas_call(
        collect_kernel,
        out_shape=pltpu.VMEM((2 * count, elems, width), F32),
        in_specs=[pl.BlockSpec(memory_space=pl.ANY)] + [vmem] * (2 * count),
        out_specs=vmem,
        compiler_params=pltpu.CompilerParams(vmem_limit_bytes=4 * MIB),
        name="collect",
    )(parts[1], *near, *far)
    came = send(crossing, tm_bit=1, rep_bit=0)
    slots = [[(n * count + k, 0) for k in range(count)] + [(2 * count, n * count + k) for k in range(count)] for n in range(2)]
    spectra = pl.pallas_call(
        functools.partial(pack_kernel, local_bins, slots),
        out_shape=pltpu.VMEM((2, elems, local_bins * lanes), F32),
        in_specs=[vmem] * (2 * count + 1),
        out_specs=vmem,
        compiler_params=pltpu.CompilerParams(vmem_limit_bytes=4 * MIB),
        name="pack",
    )(*near, *far, came)
    if each < local_bins:
        *more, inverse = prepare(1, spectra)
        parts += more
        inverses.append(inverse)
    for bit in middle:
        spectra = jnp.concatenate([spectra, send(spectra, tm_bit=0, rep_bit=bit)])
    own = jnp.concatenate([spectra, send(spectra, tm_bit=0, rep_bit=2)])
    other = jnp.concatenate([send(spectra, tm_bit=0, rep_bit=1), send(spectra, tm_bit=0, rep_bit=3)])
    bits = rep.bit_length() - 1
    proj = pl.pallas_call(
        functools.partial(first_kernel, snaps, bits),
        out_shape=pltpu.VMEM((local_bins, rows, 2 * lanes), F32),
        in_specs=[vmem] * (1 + len(parts)),
        out_specs=vmem,
        compiler_params=pltpu.CompilerParams(vmem_limit_bytes=6 * MIB),
        cost_estimate=pl.CostEstimate(flops=COST, bytes_accessed=0, transcendentals=0),
        name="first",
    )(own, *parts)
    chunk = rows // tm
    count = tm // 2
    share = pltpu.VMEM((count, chunk), F32)
    sums = [pltpu.VMEM((count, 1, chunk), F32), pltpu.VMEM((rows // 2, 2 * lanes), F32)]
    there, rights, factors = pl.pallas_call(
        functools.partial(second_kernel, elem_count, bins, snaps, bits, len(inverses)),
        out_shape=[
            share,
            pltpu.VMEM((local_bins, elem_count, 2 * lanes), BF16),
            pltpu.VMEM((local_bins, 1, 2 * lanes), F32),
        ],
        in_specs=[vmem] * (3 + len(parts) + len(inverses)),
        out_specs=[vmem] * 3,
        scratch_shapes=sums,
        compiler_params=pltpu.CompilerParams(vmem_limit_bytes=6 * MIB),
        name="second",
    )(other, own, proj, *parts, *inverses)
    here = pl.pallas_call(
        functools.partial(third_kernel, len(inverses)),
        out_shape=share,
        in_specs=[vmem] * (3 + len(parts) + len(inverses)),
        out_specs=vmem,
        scratch_shapes=sums,
        compiler_params=pltpu.CompilerParams(vmem_limit_bytes=6 * MIB),
        cost_estimate=pl.CostEstimate(flops=COST, bytes_accessed=0, transcendentals=0),
        name="third",
    )(rights, factors, proj, *parts, *inverses)
    total = here + send(there, tm_bit=count, rep_bit=0)
    for bit in bits_of(tm)[1:]:
        total = total[:bit] + send(total[bit:], tm_bit=bit, rep_bit=0)
    return total.reshape(chunk)


def solution(mesh):
    in_specs = (P("tm", "rep", None), P(), P(None, "tm", "rep", None))
    body = functools.partial(shards, mesh.shape["tm"], mesh.shape["rep"])
    return jax.shard_map(body, mesh=mesh, in_specs=in_specs, out_specs=P(("rep", "tm")), check_vma=False)
```

```python
import functools
import math

import jax
import jax.numpy as jnp
from jax import lax
from jax.experimental import pallas as pl
from jax.experimental.pallas import tpu as pltpu
from jax.sharding import PartitionSpec as P

EPS = 1e-06
F32 = jnp.float32
BF16 = jnp.bfloat16
MIB = 2**20
COST = 2 * 10**10


def dot(left, right):
    return jnp.dot(left, right, preferred_element_type=F32)


def halves(x):
    high = x.astype(BF16).astype(F32)
    return high, x - high


def dft_kernel(owners, bins_hbm, snap_hbm, keep_ref, away_ref, snap_ref, bins_ref, table_ref, sems):
    snaps, elems, samples = snap_ref.shape
    bins = bins_ref.shape[0]
    load_bins = pltpu.make_async_copy(bins_hbm, bins_ref, sems.at[0])
    load_snaps = pltpu.make_async_copy(snap_hbm, snap_ref, sems.at[1])
    load_bins.start()
    load_snaps.start()
    me = lax.axis_index("tm")
    cols = 2 * bins
    group = cols // owners
    fine = 1
    while fine * fine < samples and samples % (2 * fine) == 0:
        fine *= 2
    coarse = samples // fine
    turn = 2.0 * math.pi / samples

    def angle(count, step, freq):
        steps = lax.broadcasted_iota(jnp.int32, (count, cols), 0) * step
        return (steps * freq % samples).astype(F32) * turn

    win_c, win_f = angle(coarse, fine, 1), angle(fine, 1, 1)
    wcos_c, wsin_c = jnp.cos(win_c), jnp.sin(win_c)
    wcos_f, wsin_f = jnp.cos(win_f), jnp.sin(win_f)
    lane = lax.broadcasted_iota(jnp.int32, (1, cols), 1)
    odd = lane % 2 == 1
    bin_row = jnp.zeros((1, cols), jnp.int32)
    load_bins.wait()
    for d in range(owners):
        for f in range(group // 2):
            value = bins_ref[(me ^ d) * (group // 2) + f]
            bin_row = jnp.where(lane // 2 == d * (group // 2) + f, value, bin_row)
    angle_c, angle_f = angle(coarse, fine, bin_row), angle(fine, 1, bin_row)
    cos_c, sin_c = jnp.cos(angle_c), jnp.sin(angle_c)
    cos_f, sin_f = jnp.cos(angle_f), jnp.sin(angle_f)
    left = jnp.where(odd, -sin_c, cos_c)
    right = jnp.where(odd, cos_c, sin_c)
    for a in range(coarse):
        row = slice(a, a + 1)
        window = 0.5 - 0.5 * (wcos_c[row] * wcos_f - wsin_c[row] * wsin_f)
        high, low = halves(window * (left[row] * cos_f - right[row] * sin_f))
        table_ref[a * fine : (a + 1) * fine, :] = jnp.concatenate([high, low], axis=1).astype(BF16)
    load_snaps.wait()
    high, low = halves(snap_ref[...].reshape(snaps * elems, samples))
    product = dot(high.astype(BF16), table_ref[...]) + dot(low.astype(BF16), table_ref[...])
    spectra = product[:, :cols] + product[:, cols:]

    width = snaps * group
    source = lax.broadcasted_iota(jnp.int32, (width, width), 0)
    target = lax.broadcasted_iota(jnp.int32, (width, width), 1)
    order = jnp.where(source == target % snaps * group + target // snaps, 1.0, 0.0).astype(BF16)
    messages = jnp.concatenate(
        [
            jnp.concatenate(
                [spectra[s * elems : (s + 1) * elems, d * group : (d + 1) * group] for s in range(snaps)], axis=1
            )
            for d in range(owners)
        ],
        axis=0,
    )
    high, rest = halves(messages)
    middle, low = halves(rest)
    moved = dot(high.astype(BF16), order) + dot(middle.astype(BF16), order) + dot(low.astype(BF16), order)
    moved = moved.reshape((owners,) + keep_ref.shape[1:])
    keep_ref[...] = moved[: keep_ref.shape[0]]
    away_ref[...] = moved[keep_ref.shape[0] :]


def pack_kernel(local_bins, slots, *refs):
    *blocks, out_ref = refs
    for n in range(out_ref.shape[0]):
        parts = [blocks[k][b] for k, b in slots[n]]
        group = parts[0].shape[1] // local_bins
        out_ref[n] = jnp.concatenate(
            [part[:, f * group : (f + 1) * group] for f in range(local_bins) for part in parts], axis=1
        )


def collect_kernel(after_ref, *refs):
    del after_ref
    *blocks, out_ref = refs
    for k, block in enumerate(blocks):
        out_ref[k] = block[1]


def split_rows(elems, rep_ref, i, at, high_ref, low_ref, inverse_ref, out):
    elem_count = rep_ref.shape[3]
    step = 128 if 128 % (2 * elems) == 0 and elem_count % 128 == 0 else elem_count
    ones = jnp.ones((elem_count, inverse_ref.shape[2]), BF16)
    re, im = rep_ref[0, i, at], rep_ref[1, i, at]
    high, low = halves(re * re + im * im)
    inverse_ref[out, at] = 1.0 / (dot(high.astype(BF16), ones) + dot(low.astype(BF16), ones) + EPS)
    even = lax.broadcasted_iota(jnp.int32, (re.shape[0], step), 1) // elems % 2 == 0
    for j in range(elem_count // step):
        cut = slice(j * step, (j + 1) * step)
        real, imag = rep_ref[0, i, at, cut], rep_ref[1, i, at, cut]
        pair = (
            jnp.where(even, real, pltpu.roll(imag, elems, 1)),
            jnp.where(even, pltpu.roll(real, step - elems, 1), imag),
        )
        for a in range(2):
            high = pair[a].astype(BF16)
            high_ref[a, out, at, cut] = high
            low_ref[a, out, at, cut] = (pair[a] - high.astype(F32)).astype(BF16)


def prepare_kernel(first, elems, after_ref, rep_hbm, high_ref, low_ref, inverse_ref, *refs):
    del after_ref
    *spare, rep_ref, sems = refs
    rows = rep_ref.shape[2]
    pieces = sems.shape[2]
    tile = rows // pieces
    count = rep_ref.shape[1]

    def load(part, i, k):
        at = slice(k * tile, (k + 1) * tile)
        target = rep_ref.at[part, i, at] if i < count else spare[0].at[part, i - count, at]
        return pltpu.make_async_copy(rep_hbm.at[part, first + i, at], target, sems.at[part, i, k])

    todo = [(i, k) for i in range(sems.shape[1]) for k in range(pieces)]
    for i, k in todo:
        for part in range(2):
            load(part, i, k).start()
    for i, k in todo:
        for part in range(2):
            load(part, i, k).wait()
        if i < count:
            split_rows(elems, rep_ref, i, slice(k * tile, (k + 1) * tile), high_ref, low_ref, inverse_ref, i)


def finish_kernel(elems, after_ref, rep_ref, high_ref, low_ref, inverse_ref):
    del after_ref
    rows = rep_ref.shape[2]
    tile = math.gcd(rows, 512)
    for i in range(rep_ref.shape[1]):
        for k in range(rows // tile):
            split_rows(elems, rep_ref, i, slice(k * tile, (k + 1) * tile), high_ref, low_ref, inverse_ref, i)


def operands(spec_ref, local_bins, half, side, me, bits):
    count = spec_ref.shape[0]
    lanes = spec_ref.shape[2] // local_bins
    paired = 2 * lanes == 128 and local_bins % 2 == 0
    span = 2 * lanes if paired else lanes
    slots = []
    for p in range(count):
        apart = (2 * p + side) ^ me
        slots.append(sum(((apart >> k) & 1) * (1 << (bits - 1 - k)) for k in range(1, bits)))
    result = []
    for q in range(spec_ref.shape[2] // span):
        blocks = []
        for slot in slots:
            block = spec_ref[slot, :, q * span : (q + 1) * span]
            place = lax.broadcasted_iota(jnp.int32, block.shape, 1) % (2 * half)
            turned = jnp.where(place < half, pltpu.roll(block, span - half, 1), -pltpu.roll(block, half, 1))
            blocks += [block, turned]
        high, low = halves(jnp.concatenate(blocks, axis=0))
        if paired:
            near = lax.broadcasted_iota(jnp.int32, high.shape, 1) < lanes
            result.append(jnp.where(near, high, pltpu.roll(low, lanes, 1)).astype(BF16))
            result.append(jnp.where(near, pltpu.roll(high, lanes, 1), low).astype(BF16))
        else:
            result.append(jnp.concatenate([high, low], axis=1).astype(BF16))
    return result


def prepared(refs, axis):
    return [(ref, i) for ref in refs for i in range(ref.shape[axis])]


def first_kernel(half, bits, count, spec_ref, *refs):
    highs, lows, (proj_ref,) = prepared(refs[:count], 1), prepared(refs[count : 2 * count], 1), refs[2 * count :]
    me = lax.axis_index("rep")
    side = me & 1
    for f, right in enumerate(operands(spec_ref, proj_ref.shape[0], half, side, me, bits)):
        (high_ref, i), (low_ref, _) = highs[f], lows[f]
        proj_ref[f] = dot(high_ref[side, i], right) + dot(low_ref[side, i], right)


def rows_power(own_half, proj_ref, rights, factors, pieces, out_ref, row_ref, sum_ref):
    count, chunk = row_ref.shape[0], row_ref.shape[2]
    third = len(pieces) // 3
    highs, lows = prepared(pieces[:third], 1), prepared(pieces[third : 2 * third], 1)
    inverses = prepared(pieces[2 * third :], 0)
    lanes = proj_ref.shape[2] // 2
    side = 1 - (lax.axis_index("rep") & 1)
    owner = lax.axis_index("tm")
    top = owner // count if own_half else 1 - owner // count
    at = pl.ds(pl.multiple_of(top * count * chunk, count * chunk), count * chunk)
    for f in range(proj_ref.shape[0]):
        (high_ref, i), (low_ref, _), (inverse_ref, _) = highs[f], lows[f], inverses[f]
        proj = proj_ref[f, at] + dot(high_ref[side, i, at], rights[f])
        proj += dot(low_ref[side, i, at], rights[f])
        proj += pltpu.roll(proj, lanes, 1)
        value = proj * proj * (inverse_ref[i, at] * factors[f])
        sum_ref[...] = value if f == 0 else sum_ref[...] + value
    for k in range(count):
        row_ref[k] = jnp.sum(sum_ref[k * chunk : (k + 1) * chunk].T, axis=0, keepdims=True)
    for d in range(count):
        out_ref[d : d + 1] = row_ref[(owner ^ d) % count]


def second_kernel(elem_count, bins, half, bits, count, spec_ref, own_ref, proj_ref, *refs):
    pieces = refs[: 3 * count]
    out_ref, right_ref, factor_ref, row_ref, sum_ref = refs[3 * count :]
    local_bins = proj_ref.shape[0]
    lanes = proj_ref.shape[2] // 2
    total_snaps = lanes // 2
    me = lax.axis_index("rep")
    rights = operands(spec_ref, local_bins, half, 1 - (me & 1), me ^ 3, bits)
    squares = 0.0
    for n in range(own_ref.shape[0]):
        mine, other = own_ref[n], spec_ref[n]
        squares = squares + (mine * mine + other * other)
    squares = jnp.sum(squares, axis=0, keepdims=True)
    factors = []
    for f in range(local_bins):
        trace = jnp.sum(squares[:, f * lanes : (f + 1) * lanes], axis=1, keepdims=True) / total_snaps + EPS
        factors.append(jnp.broadcast_to(0.5 * elem_count / (trace * total_snaps * bins), factor_ref.shape[1:]))
        factor_ref[f] = factors[f]
        right_ref[f] = rights[f]
    rows_power(False, proj_ref, rights, factors, pieces, out_ref, row_ref, sum_ref)


def third_kernel(count, right_ref, factor_ref, proj_ref, *refs):
    pieces, (out_ref, row_ref, sum_ref) = refs[: 3 * count], refs[3 * count :]
    rows_power(True, proj_ref, right_ref, factor_ref, pieces, out_ref, row_ref, sum_ref)


def swap(x, mesh_shape, tm_bit, rep_bit):
    tm, rep = mesh_shape
    pairs = [(t * rep + r, (t ^ tm_bit) * rep + (r ^ rep_bit)) for t in range(tm) for r in range(rep)]
    return lax.ppermute(x, ("tm", "rep"), pairs)


def bits_of(count):
    assert count & (count - 1) == 0
    return [1 << k for k in reversed(range(count.bit_length() - 1))]


def shards(tm, rep, snapshots, freq_bins, replicas):
    snaps, elems, samples = snapshots.shape
    bins = freq_bins.shape[0]
    _, local_bins, rows, elem_count = replicas.shape
    width = 2 * local_bins * snaps
    lanes = 2 * snaps * tm
    vmem = pl.BlockSpec(memory_space=pltpu.VMEM)
    hbm = pl.BlockSpec(memory_space=pltpu.HBM)
    shape = (tm // 2, elems, width)
    keep, away = pl.pallas_call(
        functools.partial(dft_kernel, tm),
        out_shape=(pltpu.VMEM(shape, F32), pltpu.VMEM(shape, F32)),
        in_specs=[hbm, hbm],
        out_specs=[vmem] * 2,
        scratch_shapes=[
            pltpu.VMEM(snapshots.shape, F32),
            pltpu.SMEM((bins,), jnp.int32),
            pltpu.VMEM((samples, 4 * bins), BF16),
            pltpu.SemaphoreType.DMA((2,)),
        ],
        compiler_params=pltpu.CompilerParams(vmem_limit_bytes=60 * MIB),
        name="dft",
    )(freq_bins, snapshots)
    highs, lows, inverses = [], [], []
    anywhere = pl.BlockSpec(memory_space=pl.ANY)
    cost = pl.CostEstimate(flops=COST, bytes_accessed=0, transcendentals=0)
    early = -(-local_bins // 2)
    between = min(local_bins - early, -(-local_bins // 8))
    late = local_bins - early - between

    def results(count):
        shape = (2, count, rows, elem_count)
        return [pltpu.VMEM(shape, BF16), pltpu.VMEM(shape, BF16), pltpu.VMEM((count, rows, 2 * lanes), F32)]

    def add(high, low, inverse, *spare):
        highs.append(high)
        lows.append(low)
        inverses.append(inverse)
        return spare

    def prepare(count, more, limit, after):
        first = sum(part.shape[1] for part in highs)
        return add(
            *pl.pallas_call(
                functools.partial(prepare_kernel, first, elems),
                out_shape=results(count) + [pltpu.VMEM((2, more, rows, elem_count), F32)] * (more > 0),
                in_specs=[anywhere, hbm],
                out_specs=[vmem] * (3 + (more > 0)),
                scratch_shapes=[
                    pltpu.VMEM((2, count, rows, elem_count), F32),
                    pltpu.SemaphoreType.DMA((2, count + more, rows // math.gcd(rows, 512))),
                ],
                compiler_params=pltpu.CompilerParams(vmem_limit_bytes=limit * MIB),
                cost_estimate=cost,
                name="prepare",
            )(after, replicas)
        )

    def finish(spare, after):
        add(
            *pl.pallas_call(
                functools.partial(finish_kernel, elems),
                out_shape=results(spare.shape[1]),
                in_specs=[anywhere, vmem],
                out_specs=[vmem] * 3,
                compiler_params=pltpu.CompilerParams(vmem_limit_bytes=4 * MIB),
                cost_estimate=cost,
                name="finish",
            )(after, spare)
        )

    send = functools.partial(swap, mesh_shape=(tm, rep))
    held = [(keep, away)]
    spare = prepare(early, between, 38, keep)
    for bit in bits_of(tm)[:-2]:
        came = [send(b, tm_bit=bit, rep_bit=0) for _, b in held]
        kept = [a for a, _ in held] + came
        held = [(k[: bit // 2], k[bit // 2 :]) for k in kept]
    top, *middle = bits_of(rep)[:-2]
    near = [a for a, _ in held] + [send(b, tm_bit=2, rep_bit=0) for _, b in held]
    far = [send(a, tm_bit=0, rep_bit=top) for a, _ in held] + [send(b, tm_bit=2, rep_bit=top) for _, b in held]
    count = len(near)
    crossing = pl.pallas_call(
        collect_kernel,
        out_shape=pltpu.VMEM((2 * count, elems, width), F32),
        in_specs=[pl.BlockSpec(memory_space=pl.ANY)] + [vmem] * (2 * count),
        out_specs=vmem,
        compiler_params=pltpu.CompilerParams(vmem_limit_bytes=4 * MIB),
        name="collect",
    )(lows[0], *near, *far)
    if spare:
        finish(spare[0], crossing)
    came = send(crossing, tm_bit=1, rep_bit=0)
    slots = [[(n * count + k, 0) for k in range(count)] + [(2 * count, n * count + k) for k in range(count)] for n in range(2)]
    spectra = pl.pallas_call(
        functools.partial(pack_kernel, local_bins, slots),
        out_shape=pltpu.VMEM((2, elems, local_bins * lanes), F32),
        in_specs=[vmem] * (2 * count + 1),
        out_specs=vmem,
        compiler_params=pltpu.CompilerParams(vmem_limit_bytes=4 * MIB),
        name="pack",
    )(*near, *far, came)
    if late:
        prepare(late, 0, 34, spectra)
    for bit in middle:
        spectra = jnp.concatenate([spectra, send(spectra, tm_bit=0, rep_bit=bit)])
    own = jnp.concatenate([spectra, send(spectra, tm_bit=0, rep_bit=2)])
    other = jnp.concatenate([send(spectra, tm_bit=0, rep_bit=3), send(spectra, tm_bit=0, rep_bit=1)])
    bits = rep.bit_length() - 1
    proj = pl.pallas_call(
        functools.partial(first_kernel, snaps, bits, len(highs)),
        out_shape=pltpu.VMEM((local_bins, rows, 2 * lanes), F32),
        in_specs=[vmem] * (1 + 2 * len(highs)),
        out_specs=vmem,
        compiler_params=pltpu.CompilerParams(vmem_limit_bytes=6 * MIB),
        cost_estimate=pl.CostEstimate(flops=COST, bytes_accessed=0, transcendentals=0),
        name="first",
    )(own, *highs, *lows)
    chunk = rows // tm
    count = tm // 2
    share = pltpu.VMEM((count, chunk), F32)
    sums = [pltpu.VMEM((count, 1, chunk), F32), pltpu.VMEM((rows // 2, 2 * lanes), F32)]
    there, rights, factors = pl.pallas_call(
        functools.partial(second_kernel, elem_count, bins, snaps, bits, len(inverses)),
        out_shape=[
            share,
            pltpu.VMEM((local_bins, elem_count, 2 * lanes), BF16),
            pltpu.VMEM((local_bins, 1, 2 * lanes), F32),
        ],
        in_specs=[vmem] * (3 + 3 * len(highs)),
        out_specs=[vmem] * 3,
        scratch_shapes=sums,
        compiler_params=pltpu.CompilerParams(vmem_limit_bytes=6 * MIB),
        name="second",
    )(other, own, proj, *highs, *lows, *inverses)
    here = pl.pallas_call(
        functools.partial(third_kernel, len(inverses)),
        out_shape=share,
        in_specs=[vmem] * (3 + 3 * len(highs)),
        out_specs=vmem,
        scratch_shapes=sums,
        compiler_params=pltpu.CompilerParams(vmem_limit_bytes=6 * MIB),
        cost_estimate=pl.CostEstimate(flops=COST, bytes_accessed=0, transcendentals=0),
        name="third",
    )(rights, factors, proj, *highs, *lows, *inverses)
    total = here + send(there, tm_bit=count, rep_bit=0)
    for bit in bits_of(tm)[1:]:
        total = total[:bit] + send(total[bit:], tm_bit=bit, rep_bit=0)
    return total.reshape(chunk)


def solution(mesh):
    in_specs = (P("tm", "rep", None), P(), P(None, "tm", "rep", None))
    body = functools.partial(shards, mesh.shape["tm"], mesh.shape["rep"])
    return jax.shard_map(body, mesh=mesh, in_specs=in_specs, out_specs=P(("rep", "tm")), check_vma=False)
```

```python
import functools
import math

import jax
import jax.numpy as jnp
from jax import lax
from jax.experimental import pallas as pl
from jax.experimental.pallas import tpu as pltpu
from jax.sharding import PartitionSpec as P

EPS = 1e-06
F32 = jnp.float32
BF16 = jnp.bfloat16
MIB = 2**20
COST = 2 * 10**10


def dot(left, right):
    return jnp.dot(left, right, preferred_element_type=F32)


def halves(x):
    high = x.astype(BF16).astype(F32)
    return high, x - high


def dft_kernel(owners, bins_hbm, snap_hbm, keep_ref, away_ref, snap_ref, bins_ref, table_ref, sems):
    snaps, elems, samples = snap_ref.shape
    bins = bins_ref.shape[0]
    load_bins = pltpu.make_async_copy(bins_hbm, bins_ref, sems.at[0])
    load_snaps = pltpu.make_async_copy(snap_hbm, snap_ref, sems.at[1])
    load_bins.start()
    load_snaps.start()
    me = lax.axis_index("tm")
    cols = 2 * bins
    group = cols // owners
    fine = 1
    while fine * fine < samples and samples % (2 * fine) == 0:
        fine *= 2
    coarse = samples // fine
    turn = 2.0 * math.pi / samples

    def angle(count, step, freq):
        steps = lax.broadcasted_iota(jnp.int32, (count, cols), 0) * step
        return (steps * freq % samples).astype(F32) * turn

    win_c, win_f = angle(coarse, fine, 1), angle(fine, 1, 1)
    wcos_c, wsin_c = jnp.cos(win_c), jnp.sin(win_c)
    wcos_f, wsin_f = jnp.cos(win_f), jnp.sin(win_f)
    lane = lax.broadcasted_iota(jnp.int32, (1, cols), 1)
    odd = lane % 2 == 1
    bin_row = jnp.zeros((1, cols), jnp.int32)
    load_bins.wait()
    for d in range(owners):
        for f in range(group // 2):
            value = bins_ref[(me ^ d) * (group // 2) + f]
            bin_row = jnp.where(lane // 2 == d * (group // 2) + f, value, bin_row)
    angle_c, angle_f = angle(coarse, fine, bin_row), angle(fine, 1, bin_row)
    cos_c, sin_c = jnp.cos(angle_c), jnp.sin(angle_c)
    cos_f, sin_f = jnp.cos(angle_f), jnp.sin(angle_f)
    left = jnp.where(odd, -sin_c, cos_c)
    right = jnp.where(odd, cos_c, sin_c)
    for a in range(coarse):
        row = slice(a, a + 1)
        window = 0.5 - 0.5 * (wcos_c[row] * wcos_f - wsin_c[row] * wsin_f)
        high, low = halves(window * (left[row] * cos_f - right[row] * sin_f))
        table_ref[a * fine : (a + 1) * fine, :] = jnp.concatenate([high, low], axis=1).astype(BF16)
    load_snaps.wait()
    high, low = halves(snap_ref[...].reshape(snaps * elems, samples))
    product = dot(high.astype(BF16), table_ref[...]) + dot(low.astype(BF16), table_ref[...])
    spectra = product[:, :cols] + product[:, cols:]

    width = snaps * group
    source = lax.broadcasted_iota(jnp.int32, (width, width), 0)
    target = lax.broadcasted_iota(jnp.int32, (width, width), 1)
    order = jnp.where(source == target % snaps * group + target // snaps, 1.0, 0.0).astype(BF16)
    messages = jnp.concatenate(
        [
            jnp.concatenate(
                [spectra[s * elems : (s + 1) * elems, d * group : (d + 1) * group] for s in range(snaps)], axis=1
            )
            for d in range(owners)
        ],
        axis=0,
    )
    high, rest = halves(messages)
    middle, low = halves(rest)
    moved = dot(high.astype(BF16), order) + dot(middle.astype(BF16), order) + dot(low.astype(BF16), order)
    moved = moved.reshape((owners,) + keep_ref.shape[1:])
    keep_ref[...] = moved[: keep_ref.shape[0]]
    away_ref[...] = moved[keep_ref.shape[0] :]


def interleave(parts, local_bins):
    width = parts[0].shape[1]
    group = width // local_bins
    fits = width == 128 and len(parts) * 2 * group == width and local_bins % 2 == 0
    if not fits or len(parts) & (len(parts) - 1):
        return jnp.concatenate(
            [part[:, f * group : (f + 1) * group] for f in range(local_bins) for part in parts], axis=1
        )
    lane = lax.broadcasted_iota(jnp.int32, parts[0].shape, 1)
    merged, size = [{None: (part, list(range(local_bins)))} for part in parts], group
    while len(merged) > 1:
        even = lane // size % 2 == 0
        following = []
        for a, b in zip(merged[::2], merged[1::2]):
            both = {}
            for key in a:
                (x, bins), (y, _) = a[key], b[key]
                both[key, 0] = jnp.where(even, x, pltpu.roll(y, size, 1)), bins[::2]
                both[key, 1] = jnp.where(even, pltpu.roll(x, width - size, 1), y), bins[1::2]
            following.append(both)
        merged, size = following, 2 * size
    place = {f: (x, k) for x, bins in merged[0].values() for k, f in enumerate(bins)}
    near = lane < size
    pairs = []
    for f in range(0, local_bins, 2):
        (x, i), (y, j) = place[f], place[f + 1]
        pairs.append(jnp.where(near, pltpu.roll(x, size, 1) if i else x, y if j else pltpu.roll(y, size, 1)))
    return jnp.concatenate(pairs, axis=1)


def pack_kernel(local_bins, slots, *refs):
    *blocks, out_ref = refs
    for n in range(out_ref.shape[0]):
        out_ref[n] = interleave([blocks[k][b] for k, b in slots[n]], local_bins)


def collect_kernel(after_ref, *refs):
    del after_ref
    *blocks, out_ref = refs
    for k, block in enumerate(blocks):
        out_ref[k] = block[1]


def split_rows(elems, rep_ref, i, at, high_ref, low_ref, inverse_ref, out):
    elem_count = rep_ref.shape[3]
    step = 128 if 128 % (2 * elems) == 0 and elem_count % 128 == 0 else elem_count
    ones = jnp.ones((elem_count, inverse_ref.shape[2]), BF16)
    re, im = rep_ref[0, i, at], rep_ref[1, i, at]
    high, low = halves(re * re + im * im)
    inverse_ref[out, at] = 1.0 / (dot(high.astype(BF16), ones) + dot(low.astype(BF16), ones) + EPS)
    even = lax.broadcasted_iota(jnp.int32, (re.shape[0], step), 1) // elems % 2 == 0
    for j in range(elem_count // step):
        cut = slice(j * step, (j + 1) * step)
        real, imag = rep_ref[0, i, at, cut], rep_ref[1, i, at, cut]
        pair = (
            jnp.where(even, real, pltpu.roll(imag, elems, 1)),
            jnp.where(even, pltpu.roll(real, step - elems, 1), imag),
        )
        for a in range(2):
            high = pair[a].astype(BF16)
            high_ref[a, out, at, cut] = high
            low_ref[a, out, at, cut] = (pair[a] - high.astype(F32)).astype(BF16)


def prepare_kernel(first, elems, after_ref, rep_hbm, high_ref, low_ref, inverse_ref, *refs):
    del after_ref
    *spare, rep_ref, sems = refs
    rows = rep_ref.shape[2]
    pieces = sems.shape[2]
    tile = rows // pieces
    count = rep_ref.shape[1]

    def load(part, i, k):
        at = slice(k * tile, (k + 1) * tile)
        target = rep_ref.at[part, i, at] if i < count else spare[0].at[part, i - count, at]
        return pltpu.make_async_copy(rep_hbm.at[part, first + i, at], target, sems.at[part, i, k])

    todo = [(i, k) for i in range(sems.shape[1]) for k in range(pieces)]
    for i, k in todo:
        for part in range(2):
            load(part, i, k).start()
    for i, k in todo:
        for part in range(2):
            load(part, i, k).wait()
        if i < count:
            split_rows(elems, rep_ref, i, slice(k * tile, (k + 1) * tile), high_ref, low_ref, inverse_ref, i)


def finish_kernel(elems, after_ref, rep_ref, high_ref, low_ref, inverse_ref):
    del after_ref
    rows = rep_ref.shape[2]
    tile = math.gcd(rows, 512)
    for i in range(rep_ref.shape[1]):
        for k in range(rows // tile):
            split_rows(elems, rep_ref, i, slice(k * tile, (k + 1) * tile), high_ref, low_ref, inverse_ref, i)


def operands(spec_ref, local_bins, half, side, me, bits):
    count = spec_ref.shape[0]
    lanes = spec_ref.shape[2] // local_bins
    paired = 2 * lanes == 128 and local_bins % 2 == 0
    span = 2 * lanes if paired else lanes
    slots = []
    for p in range(count):
        apart = (2 * p + side) ^ me
        slots.append(sum(((apart >> k) & 1) * (1 << (bits - 1 - k)) for k in range(1, bits)))
    result = []
    for q in range(spec_ref.shape[2] // span):
        blocks = []
        for slot in slots:
            block = spec_ref[slot, :, q * span : (q + 1) * span]
            place = lax.broadcasted_iota(jnp.int32, block.shape, 1) % (2 * half)
            turned = jnp.where(place < half, pltpu.roll(block, span - half, 1), -pltpu.roll(block, half, 1))
            blocks += [block, turned]
        high, low = halves(jnp.concatenate(blocks, axis=0))
        if paired:
            near = lax.broadcasted_iota(jnp.int32, high.shape, 1) < lanes
            result.append(jnp.where(near, high, pltpu.roll(low, lanes, 1)).astype(BF16))
            result.append(jnp.where(near, pltpu.roll(high, lanes, 1), low).astype(BF16))
        else:
            result.append(jnp.concatenate([high, low], axis=1).astype(BF16))
    return result


def prepared(refs, axis):
    return [(ref, i) for ref in refs for i in range(ref.shape[axis])]


def first_kernel(half, bits, count, spec_ref, *refs):
    highs, lows, (proj_ref,) = prepared(refs[:count], 1), prepared(refs[count : 2 * count], 1), refs[2 * count :]
    me = lax.axis_index("rep")
    side = me & 1
    for f, right in enumerate(operands(spec_ref, proj_ref.shape[0], half, side, me, bits)):
        (high_ref, i), (low_ref, _) = highs[f], lows[f]
        proj_ref[f] = dot(high_ref[side, i], right) + dot(low_ref[side, i], right)


def rows_power(own_half, proj_ref, rights, factors, pieces, out_ref, row_ref, sum_ref):
    count, chunk = row_ref.shape[0], row_ref.shape[2]
    third = len(pieces) // 3
    highs, lows = prepared(pieces[:third], 1), prepared(pieces[third : 2 * third], 1)
    inverses = prepared(pieces[2 * third :], 0)
    lanes = proj_ref.shape[2] // 2
    side = 1 - (lax.axis_index("rep") & 1)
    owner = lax.axis_index("tm")
    top = owner // count if own_half else 1 - owner // count
    at = pl.ds(pl.multiple_of(top * count * chunk, count * chunk), count * chunk)
    for f in range(proj_ref.shape[0]):
        (high_ref, i), (low_ref, _), (inverse_ref, _) = highs[f], lows[f], inverses[f]
        proj = proj_ref[f, at] + dot(high_ref[side, i, at], rights[f])
        proj += dot(low_ref[side, i, at], rights[f])
        proj += pltpu.roll(proj, lanes, 1)
        value = proj * proj * (inverse_ref[i, at] * factors[f])
        sum_ref[...] = value if f == 0 else sum_ref[...] + value
    for k in range(count):
        row_ref[k] = jnp.sum(sum_ref[k * chunk : (k + 1) * chunk].T, axis=0, keepdims=True)
    for d in range(count):
        out_ref[d : d + 1] = row_ref[(owner ^ d) % count]


def second_kernel(elem_count, bins, half, bits, count, spec_ref, own_ref, proj_ref, *refs):
    pieces = refs[: 3 * count]
    out_ref, right_ref, factor_ref, row_ref, sum_ref = refs[3 * count :]
    local_bins = proj_ref.shape[0]
    lanes = proj_ref.shape[2] // 2
    total_snaps = lanes // 2
    me = lax.axis_index("rep")
    rights = operands(spec_ref, local_bins, half, 1 - (me & 1), me ^ 3, bits)
    squares = 0.0
    for n in range(own_ref.shape[0]):
        mine, other = own_ref[n], spec_ref[n]
        squares = squares + (mine * mine + other * other)
    squares = jnp.sum(squares, axis=0, keepdims=True)
    factors = []
    for f in range(local_bins):
        trace = jnp.sum(squares[:, f * lanes : (f + 1) * lanes], axis=1, keepdims=True) / total_snaps + EPS
        factors.append(jnp.broadcast_to(0.5 * elem_count / (trace * total_snaps * bins), factor_ref.shape[1:]))
        factor_ref[f] = factors[f]
        right_ref[f] = rights[f]
    rows_power(False, proj_ref, rights, factors, pieces, out_ref, row_ref, sum_ref)


def third_kernel(count, right_ref, factor_ref, proj_ref, *refs):
    pieces, (out_ref, row_ref, sum_ref) = refs[: 3 * count], refs[3 * count :]
    rows_power(True, proj_ref, right_ref, factor_ref, pieces, out_ref, row_ref, sum_ref)


def swap(x, mesh_shape, tm_bit, rep_bit):
    tm, rep = mesh_shape
    pairs = [(t * rep + r, (t ^ tm_bit) * rep + (r ^ rep_bit)) for t in range(tm) for r in range(rep)]
    return lax.ppermute(x, ("tm", "rep"), pairs)


def bits_of(count):
    assert count & (count - 1) == 0
    return [1 << k for k in reversed(range(count.bit_length() - 1))]


def shards(tm, rep, snapshots, freq_bins, replicas):
    snaps, elems, samples = snapshots.shape
    bins = freq_bins.shape[0]
    _, local_bins, rows, elem_count = replicas.shape
    width = 2 * local_bins * snaps
    lanes = 2 * snaps * tm
    vmem = pl.BlockSpec(memory_space=pltpu.VMEM)
    hbm = pl.BlockSpec(memory_space=pltpu.HBM)
    shape = (tm // 2, elems, width)
    keep, away = pl.pallas_call(
        functools.partial(dft_kernel, tm),
        out_shape=(pltpu.VMEM(shape, F32), pltpu.VMEM(shape, F32)),
        in_specs=[hbm, hbm],
        out_specs=[vmem] * 2,
        scratch_shapes=[
            pltpu.VMEM(snapshots.shape, F32),
            pltpu.SMEM((bins,), jnp.int32),
            pltpu.VMEM((samples, 4 * bins), BF16),
            pltpu.SemaphoreType.DMA((2,)),
        ],
        compiler_params=pltpu.CompilerParams(vmem_limit_bytes=60 * MIB),
        name="dft",
    )(freq_bins, snapshots)
    highs, lows, inverses = [], [], []
    anywhere = pl.BlockSpec(memory_space=pl.ANY)
    cost = pl.CostEstimate(flops=COST, bytes_accessed=0, transcendentals=0)
    early = -(-local_bins // 2)
    between = min(local_bins - early, -(-local_bins // 8))
    late = local_bins - early - between

    def results(count):
        shape = (2, count, rows, elem_count)
        return [pltpu.VMEM(shape, BF16), pltpu.VMEM(shape, BF16), pltpu.VMEM((count, rows, 2 * lanes), F32)]

    def add(high, low, inverse, *spare):
        highs.append(high)
        lows.append(low)
        inverses.append(inverse)
        return spare

    def prepare(count, more, limit, after):
        first = sum(part.shape[1] for part in highs)
        return add(
            *pl.pallas_call(
                functools.partial(prepare_kernel, first, elems),
                out_shape=results(count) + [pltpu.VMEM((2, more, rows, elem_count), F32)] * (more > 0),
                in_specs=[anywhere, hbm],
                out_specs=[vmem] * (3 + (more > 0)),
                scratch_shapes=[
                    pltpu.VMEM((2, count, rows, elem_count), F32),
                    pltpu.SemaphoreType.DMA((2, count + more, rows // math.gcd(rows, 512))),
                ],
                compiler_params=pltpu.CompilerParams(vmem_limit_bytes=limit * MIB),
                cost_estimate=cost,
                name="prepare",
            )(after, replicas)
        )

    def finish(spare, after):
        add(
            *pl.pallas_call(
                functools.partial(finish_kernel, elems),
                out_shape=results(spare.shape[1]),
                in_specs=[anywhere, vmem],
                out_specs=[vmem] * 3,
                compiler_params=pltpu.CompilerParams(vmem_limit_bytes=4 * MIB),
                cost_estimate=cost,
                name="finish",
            )(after, spare)
        )

    send = functools.partial(swap, mesh_shape=(tm, rep))
    held = [(keep, away)]
    spare = prepare(early, between, 38, keep)
    for bit in bits_of(tm)[:-2]:
        came = [send(b, tm_bit=bit, rep_bit=0) for _, b in held]
        kept = [a for a, _ in held] + came
        held = [(k[: bit // 2], k[bit // 2 :]) for k in kept]
    top, *middle = bits_of(rep)[:-2]
    near = [a for a, _ in held] + [send(b, tm_bit=2, rep_bit=0) for _, b in held]
    far = [send(a, tm_bit=0, rep_bit=top) for a, _ in held] + [send(b, tm_bit=2, rep_bit=top) for _, b in held]
    count = len(near)
    crossing = pl.pallas_call(
        collect_kernel,
        out_shape=pltpu.VMEM((2 * count, elems, width), F32),
        in_specs=[pl.BlockSpec(memory_space=pl.ANY)] + [vmem] * (2 * count),
        out_specs=vmem,
        compiler_params=pltpu.CompilerParams(vmem_limit_bytes=4 * MIB),
        name="collect",
    )(lows[0], *near, *far)
    if spare:
        finish(spare[0], crossing)
    came = send(crossing, tm_bit=1, rep_bit=0)
    slots = [[(n * count + k, 0) for k in range(count)] + [(2 * count, n * count + k) for k in range(count)] for n in range(2)]
    spectra = pl.pallas_call(
        functools.partial(pack_kernel, local_bins, slots),
        out_shape=pltpu.VMEM((2, elems, local_bins * lanes), F32),
        in_specs=[vmem] * (2 * count + 1),
        out_specs=vmem,
        compiler_params=pltpu.CompilerParams(vmem_limit_bytes=4 * MIB),
        name="pack",
    )(*near, *far, came)
    if late:
        prepare(late, 0, 34, spectra)
    for bit in middle:
        spectra = jnp.concatenate([spectra, send(spectra, tm_bit=0, rep_bit=bit)])
    own = jnp.concatenate([spectra, send(spectra, tm_bit=0, rep_bit=2)])
    other = jnp.concatenate([send(spectra, tm_bit=0, rep_bit=3), send(spectra, tm_bit=0, rep_bit=1)])
    bits = rep.bit_length() - 1
    proj = pl.pallas_call(
        functools.partial(first_kernel, snaps, bits, len(highs)),
        out_shape=pltpu.VMEM((local_bins, rows, 2 * lanes), F32),
        in_specs=[vmem] * (1 + 2 * len(highs)),
        out_specs=vmem,
        compiler_params=pltpu.CompilerParams(vmem_limit_bytes=6 * MIB),
        cost_estimate=pl.CostEstimate(flops=COST, bytes_accessed=0, transcendentals=0),
        name="first",
    )(own, *highs, *lows)
    chunk = rows // tm
    count = tm // 2
    share = pltpu.VMEM((count, chunk), F32)
    sums = [pltpu.VMEM((count, 1, chunk), F32), pltpu.VMEM((rows // 2, 2 * lanes), F32)]
    there, rights, factors = pl.pallas_call(
        functools.partial(second_kernel, elem_count, bins, snaps, bits, len(inverses)),
        out_shape=[
            share,
            pltpu.VMEM((local_bins, elem_count, 2 * lanes), BF16),
            pltpu.VMEM((local_bins, 1, 2 * lanes), F32),
        ],
        in_specs=[vmem] * (3 + 3 * len(highs)),
        out_specs=[vmem] * 3,
        scratch_shapes=sums,
        compiler_params=pltpu.CompilerParams(vmem_limit_bytes=6 * MIB),
        name="second",
    )(other, own, proj, *highs, *lows, *inverses)
    here = pl.pallas_call(
        functools.partial(third_kernel, len(inverses)),
        out_shape=share,
        in_specs=[vmem] * (3 + 3 * len(highs)),
        out_specs=vmem,
        scratch_shapes=sums,
        compiler_params=pltpu.CompilerParams(vmem_limit_bytes=6 * MIB),
        cost_estimate=pl.CostEstimate(flops=COST, bytes_accessed=0, transcendentals=0),
        name="third",
    )(rights, factors, proj, *highs, *lows, *inverses)
    total = here + send(there, tm_bit=count, rep_bit=0)
    for bit in bits_of(tm)[1:]:
        total = total[:bit] + send(total[bit:], tm_bit=bit, rep_bit=0)
    return total.reshape(chunk)


def solution(mesh):
    in_specs = (P("tm", "rep", None), P(), P(None, "tm", "rep", None))
    body = functools.partial(shards, mesh.shape["tm"], mesh.shape["rep"])
    return jax.shard_map(body, mesh=mesh, in_specs=in_specs, out_specs=P(("rep", "tm")), check_vma=False)
```

```python
import functools
import math

import jax
import jax.numpy as jnp
from jax import lax
from jax.experimental import pallas as pl
from jax.experimental.pallas import tpu as pltpu
from jax.sharding import PartitionSpec as P

EPS = 1e-06
F32 = jnp.float32
BF16 = jnp.bfloat16
MIB = 2**20
COST = 2 * 10**10


def dot(left, right):
    return jnp.dot(left, right, preferred_element_type=F32)


def halves(x):
    high = x.astype(BF16).astype(F32)
    return high, x - high


def dft_kernel(owners, bins_hbm, snap_hbm, keep_ref, away_ref, snap_ref, bins_ref, table_ref, sems):
    snaps, elems, samples = snap_ref.shape
    bins = bins_ref.shape[0]
    load_bins = pltpu.make_async_copy(bins_hbm, bins_ref, sems.at[0])
    load_snaps = pltpu.make_async_copy(snap_hbm, snap_ref, sems.at[1])
    load_snaps.start()
    load_bins.start()
    me = lax.axis_index("tm")
    cols = 2 * bins
    group = cols // owners
    fine = 1
    while fine * fine < samples and samples % (2 * fine) == 0:
        fine *= 2
    coarse = samples // fine
    turn = 2.0 * math.pi / samples

    def angle(count, step, freq):
        steps = lax.broadcasted_iota(jnp.int32, (count, cols), 0) * step
        return (steps * freq % samples).astype(F32) * turn

    win_c, win_f = angle(coarse, fine, 1), angle(fine, 1, 1)
    wcos_c, wsin_c = jnp.cos(win_c), jnp.sin(win_c)
    wcos_f, wsin_f = jnp.cos(win_f), jnp.sin(win_f)
    lane = lax.broadcasted_iota(jnp.int32, (1, cols), 1)
    odd = lane % 2 == 1
    bin_row = jnp.zeros((1, cols), jnp.int32)
    load_bins.wait()
    for d in range(owners):
        for f in range(group // 2):
            value = bins_ref[(me ^ d) * (group // 2) + f]
            bin_row = jnp.where(lane // 2 == d * (group // 2) + f, value, bin_row)
    angle_c, angle_f = angle(coarse, fine, bin_row), angle(fine, 1, bin_row)
    cos_c, sin_c = jnp.cos(angle_c), jnp.sin(angle_c)
    cos_f, sin_f = jnp.cos(angle_f), jnp.sin(angle_f)
    left = jnp.where(odd, -sin_c, cos_c)
    right = jnp.where(odd, cos_c, sin_c)
    for a in range(coarse):
        row = slice(a, a + 1)
        window = 0.5 - 0.5 * (wcos_c[row] * wcos_f - wsin_c[row] * wsin_f)
        high, low = halves(window * (left[row] * cos_f - right[row] * sin_f))
        table_ref[a * fine : (a + 1) * fine, :] = jnp.concatenate([high, low], axis=1).astype(BF16)
    load_snaps.wait()
    high, low = halves(snap_ref[...].reshape(snaps * elems, samples))
    product = dot(high.astype(BF16), table_ref[...]) + dot(low.astype(BF16), table_ref[...])
    spectra = product[:, :cols] + product[:, cols:]

    width = snaps * group
    source = lax.broadcasted_iota(jnp.int32, (width, width), 0)
    target = lax.broadcasted_iota(jnp.int32, (width, width), 1)
    order = jnp.where(source == target % snaps * group + target // snaps, 1.0, 0.0).astype(BF16)
    messages = jnp.concatenate(
        [
            jnp.concatenate(
                [spectra[s * elems : (s + 1) * elems, d * group : (d + 1) * group] for s in range(snaps)], axis=1
            )
            for d in range(owners)
        ],
        axis=0,
    )
    high, rest = halves(messages)
    middle, low = halves(rest)
    moved = dot(high.astype(BF16), order) + dot(middle.astype(BF16), order) + dot(low.astype(BF16), order)
    moved = moved.reshape((owners,) + keep_ref.shape[1:])
    keep_ref[...] = moved[: keep_ref.shape[0]]
    away_ref[...] = moved[keep_ref.shape[0] :]


def interleave(parts, local_bins):
    width = parts[0].shape[1]
    group = width // local_bins
    fits = width == 128 and len(parts) * 2 * group == width and local_bins % 2 == 0
    if not fits or len(parts) & (len(parts) - 1):
        return jnp.concatenate(
            [part[:, f * group : (f + 1) * group] for f in range(local_bins) for part in parts], axis=1
        )
    lane = lax.broadcasted_iota(jnp.int32, parts[0].shape, 1)
    merged, size = [{None: (part, list(range(local_bins)))} for part in parts], group
    while len(merged) > 1:
        even = lane // size % 2 == 0
        following = []
        for a, b in zip(merged[::2], merged[1::2]):
            both = {}
            for key in a:
                (x, bins), (y, _) = a[key], b[key]
                both[key, 0] = jnp.where(even, x, pltpu.roll(y, size, 1)), bins[::2]
                both[key, 1] = jnp.where(even, pltpu.roll(x, width - size, 1), y), bins[1::2]
            following.append(both)
        merged, size = following, 2 * size
    place = {f: (x, k) for x, bins in merged[0].values() for k, f in enumerate(bins)}
    near = lane < size
    pairs = []
    for f in range(0, local_bins, 2):
        (x, i), (y, j) = place[f], place[f + 1]
        pairs.append(jnp.where(near, pltpu.roll(x, size, 1) if i else x, y if j else pltpu.roll(y, size, 1)))
    return jnp.concatenate(pairs, axis=1)


def pack_kernel(local_bins, slots, *refs):
    *blocks, out_ref = refs
    for n in range(out_ref.shape[0]):
        out_ref[n] = interleave([blocks[k][b] for k, b in slots[n]], local_bins)


def collect_kernel(after_ref, *refs):
    del after_ref
    *blocks, out_ref = refs
    for k, block in enumerate(blocks):
        out_ref[k] = block[1]


def split_rows(elems, rep_ref, i, at, high_ref, low_ref, inverse_ref, out):
    elem_count = rep_ref.shape[3]
    step = 128 if 128 % (2 * elems) == 0 and elem_count % 128 == 0 else elem_count
    ones = jnp.ones((elem_count, inverse_ref.shape[2]), BF16)
    re, im = rep_ref[0, i, at], rep_ref[1, i, at]
    high, low = halves(re * re + im * im)
    inverse_ref[out, at] = 1.0 / (dot(high.astype(BF16), ones) + dot(low.astype(BF16), ones) + EPS)
    even = lax.broadcasted_iota(jnp.int32, (re.shape[0], step), 1) // elems % 2 == 0
    for j in range(elem_count // step):
        cut = slice(j * step, (j + 1) * step)
        real, imag = rep_ref[0, i, at, cut], rep_ref[1, i, at, cut]
        pair = (
            jnp.where(even, real, pltpu.roll(imag, elems, 1)),
            jnp.where(even, pltpu.roll(real, step - elems, 1), imag),
        )
        for a in range(2):
            high = pair[a].astype(BF16)
            high_ref[a, out, at, cut] = high
            low_ref[a, out, at, cut] = (pair[a] - high.astype(F32)).astype(BF16)


def prepare_kernel(first, elems, after_ref, rep_hbm, high_ref, low_ref, inverse_ref, *refs):
    del after_ref
    *spare, rep_ref, sems = refs
    rows = rep_ref.shape[2]
    pieces = sems.shape[2]
    tile = rows // pieces
    count = rep_ref.shape[1]

    def load(part, i, k):
        at = slice(k * tile, (k + 1) * tile)
        target = rep_ref.at[part, i, at] if i < count else spare[0].at[part, i - count, at]
        return pltpu.make_async_copy(rep_hbm.at[part, first + i, at], target, sems.at[part, i, k])

    todo = [(i, k) for i in range(sems.shape[1]) for k in range(pieces)]
    for i, k in todo:
        for part in range(2):
            load(part, i, k).start()
    for i, k in todo:
        for part in range(2):
            load(part, i, k).wait()
        if i < count:
            split_rows(elems, rep_ref, i, slice(k * tile, (k + 1) * tile), high_ref, low_ref, inverse_ref, i)


def finish_kernel(elems, after_ref, rep_ref, high_ref, low_ref, inverse_ref):
    del after_ref
    rows = rep_ref.shape[2]
    tile = math.gcd(rows, 512)
    for i in range(rep_ref.shape[1]):
        for k in range(rows // tile):
            split_rows(elems, rep_ref, i, slice(k * tile, (k + 1) * tile), high_ref, low_ref, inverse_ref, i)


def operands(spec_ref, local_bins, half, side, me, bits):
    count = spec_ref.shape[0]
    lanes = spec_ref.shape[2] // local_bins
    paired = 2 * lanes == 128 and local_bins % 2 == 0
    span = 2 * lanes if paired else lanes
    slots = []
    for p in range(count):
        apart = (2 * p + side) ^ me
        slots.append(sum(((apart >> k) & 1) * (1 << (bits - 1 - k)) for k in range(1, bits)))
    result = []
    for q in range(spec_ref.shape[2] // span):
        blocks = []
        for slot in slots:
            block = spec_ref[slot, :, q * span : (q + 1) * span]
            place = lax.broadcasted_iota(jnp.int32, block.shape, 1) % (2 * half)
            turned = jnp.where(place < half, pltpu.roll(block, span - half, 1), -pltpu.roll(block, half, 1))
            blocks += [block, turned]
        high, low = halves(jnp.concatenate(blocks, axis=0))
        if paired:
            near = lax.broadcasted_iota(jnp.int32, high.shape, 1) < lanes
            result.append(jnp.where(near, high, pltpu.roll(low, lanes, 1)).astype(BF16))
            result.append(jnp.where(near, pltpu.roll(high, lanes, 1), low).astype(BF16))
        else:
            result.append(jnp.concatenate([high, low], axis=1).astype(BF16))
    return result


def prepared(refs, axis):
    return [(ref, i) for ref in refs for i in range(ref.shape[axis])]


def first_kernel(half, bits, count, spec_ref, *refs):
    highs, lows, (proj_ref,) = prepared(refs[:count], 1), prepared(refs[count : 2 * count], 1), refs[2 * count :]
    me = lax.axis_index("rep")
    side = me & 1
    for f, right in enumerate(operands(spec_ref, proj_ref.shape[0], half, side, me, bits)):
        (high_ref, i), (low_ref, _) = highs[f], lows[f]
        proj_ref[f] = dot(high_ref[side, i], right) + dot(low_ref[side, i], right)


def rows_power(own_half, proj_ref, rights, factors, pieces, out_ref, row_ref, sum_ref):
    count, chunk = row_ref.shape[0], row_ref.shape[2]
    third = len(pieces) // 3
    highs, lows = prepared(pieces[:third], 1), prepared(pieces[third : 2 * third], 1)
    inverses = prepared(pieces[2 * third :], 0)
    lanes = proj_ref.shape[2] // 2
    side = 1 - (lax.axis_index("rep") & 1)
    owner = lax.axis_index("tm")
    top = owner // count if own_half else 1 - owner // count
    at = pl.ds(pl.multiple_of(top * count * chunk, count * chunk), count * chunk)
    for f in range(proj_ref.shape[0]):
        (high_ref, i), (low_ref, _), (inverse_ref, _) = highs[f], lows[f], inverses[f]
        proj = proj_ref[f, at] + dot(high_ref[side, i, at], rights[f])
        proj += dot(low_ref[side, i, at], rights[f])
        proj += pltpu.roll(proj, lanes, 1)
        value = proj * proj * (inverse_ref[i, at] * factors[f])
        sum_ref[...] = value if f == 0 else sum_ref[...] + value
    for k in range(count):
        row_ref[k] = jnp.sum(sum_ref[k * chunk : (k + 1) * chunk].T, axis=0, keepdims=True)
    for d in range(count):
        out_ref[d : d + 1] = row_ref[(owner ^ d) % count]


def second_kernel(elem_count, bins, half, bits, count, spec_ref, own_ref, proj_ref, *refs):
    pieces = refs[: 3 * count]
    out_ref, right_ref, factor_ref, row_ref, sum_ref = refs[3 * count :]
    local_bins = proj_ref.shape[0]
    lanes = proj_ref.shape[2] // 2
    total_snaps = lanes // 2
    me = lax.axis_index("rep")
    rights = operands(spec_ref, local_bins, half, 1 - (me & 1), me ^ 3, bits)
    squares = 0.0
    for n in range(own_ref.shape[0]):
        mine, other = own_ref[n], spec_ref[n]
        squares = squares + (mine * mine + other * other)
    squares = jnp.sum(squares, axis=0, keepdims=True)
    factors = []
    for f in range(local_bins):
        trace = jnp.sum(squares[:, f * lanes : (f + 1) * lanes], axis=1, keepdims=True) / total_snaps + EPS
        factors.append(jnp.broadcast_to(0.5 * elem_count / (trace * total_snaps * bins), factor_ref.shape[1:]))
        factor_ref[f] = factors[f]
        right_ref[f] = rights[f]
    rows_power(False, proj_ref, rights, factors, pieces, out_ref, row_ref, sum_ref)


def third_kernel(count, right_ref, factor_ref, proj_ref, *refs):
    pieces, (out_ref, row_ref, sum_ref) = refs[: 3 * count], refs[3 * count :]
    rows_power(True, proj_ref, right_ref, factor_ref, pieces, out_ref, row_ref, sum_ref)


def swap(x, mesh_shape, tm_bit, rep_bit):
    tm, rep = mesh_shape
    pairs = [(t * rep + r, (t ^ tm_bit) * rep + (r ^ rep_bit)) for t in range(tm) for r in range(rep)]
    return lax.ppermute(x, ("tm", "rep"), pairs)


def bits_of(count):
    assert count & (count - 1) == 0
    return [1 << k for k in reversed(range(count.bit_length() - 1))]


def shards(tm, rep, snapshots, freq_bins, replicas):
    snaps, elems, samples = snapshots.shape
    bins = freq_bins.shape[0]
    _, local_bins, rows, elem_count = replicas.shape
    width = 2 * local_bins * snaps
    lanes = 2 * snaps * tm
    vmem = pl.BlockSpec(memory_space=pltpu.VMEM)
    hbm = pl.BlockSpec(memory_space=pltpu.HBM)
    shape = (tm // 2, elems, width)
    keep, away = pl.pallas_call(
        functools.partial(dft_kernel, tm),
        out_shape=(pltpu.VMEM(shape, F32), pltpu.VMEM(shape, F32)),
        in_specs=[hbm, hbm],
        out_specs=[vmem] * 2,
        scratch_shapes=[
            pltpu.VMEM(snapshots.shape, F32),
            pltpu.SMEM((bins,), jnp.int32),
            pltpu.VMEM((samples, 4 * bins), BF16),
            pltpu.SemaphoreType.DMA((2,)),
        ],
        compiler_params=pltpu.CompilerParams(vmem_limit_bytes=60 * MIB),
        name="dft",
    )(freq_bins, snapshots)
    highs, lows, inverses = [], [], []
    anywhere = pl.BlockSpec(memory_space=pl.ANY)
    cost = pl.CostEstimate(flops=COST, bytes_accessed=0, transcendentals=0)
    early = -(-local_bins // 2)
    between = min(local_bins - early, -(-local_bins // 8))
    late = local_bins - early - between

    def results(count):
        shape = (2, count, rows, elem_count)
        return [pltpu.VMEM(shape, BF16), pltpu.VMEM(shape, BF16), pltpu.VMEM((count, rows, 2 * lanes), F32)]

    def add(high, low, inverse, *spare):
        highs.append(high)
        lows.append(low)
        inverses.append(inverse)
        return spare

    def prepare(count, more, limit, after):
        first = sum(part.shape[1] for part in highs)
        return add(
            *pl.pallas_call(
                functools.partial(prepare_kernel, first, elems),
                out_shape=results(count) + [pltpu.VMEM((2, more, rows, elem_count), F32)] * (more > 0),
                in_specs=[anywhere, hbm],
                out_specs=[vmem] * (3 + (more > 0)),
                scratch_shapes=[
                    pltpu.VMEM((2, count, rows, elem_count), F32),
                    pltpu.SemaphoreType.DMA((2, count + more, rows // math.gcd(rows, 512))),
                ],
                compiler_params=pltpu.CompilerParams(vmem_limit_bytes=limit * MIB),
                cost_estimate=cost,
                name="prepare",
            )(after, replicas)
        )

    def finish(spare, after):
        add(
            *pl.pallas_call(
                functools.partial(finish_kernel, elems),
                out_shape=results(spare.shape[1]),
                in_specs=[anywhere, vmem],
                out_specs=[vmem] * 3,
                compiler_params=pltpu.CompilerParams(vmem_limit_bytes=4 * MIB),
                cost_estimate=cost,
                name="finish",
            )(after, spare)
        )

    send = functools.partial(swap, mesh_shape=(tm, rep))
    held = [(keep, away)]
    spare = prepare(early, between, 38, keep)
    for bit in bits_of(tm)[:-2]:
        came = [send(b, tm_bit=bit, rep_bit=0) for _, b in held]
        kept = [a for a, _ in held] + came
        held = [(k[: bit // 2], k[bit // 2 :]) for k in kept]
    top, *middle = bits_of(rep)[:-2]
    near = [a for a, _ in held] + [send(b, tm_bit=2, rep_bit=0) for _, b in held]
    far = [send(a, tm_bit=0, rep_bit=top) for a, _ in held] + [send(b, tm_bit=2, rep_bit=top) for _, b in held]
    count = len(near)
    crossing = pl.pallas_call(
        collect_kernel,
        out_shape=pltpu.VMEM((2 * count, elems, width), F32),
        in_specs=[pl.BlockSpec(memory_space=pl.ANY)] + [vmem] * (2 * count),
        out_specs=vmem,
        compiler_params=pltpu.CompilerParams(vmem_limit_bytes=4 * MIB),
        name="collect",
    )(lows[0], *near, *far)
    if spare:
        finish(spare[0], crossing)
    came = send(crossing, tm_bit=1, rep_bit=0)
    slots = [[(n * count + k, 0) for k in range(count)] + [(2 * count, n * count + k) for k in range(count)] for n in range(2)]
    spectra = pl.pallas_call(
        functools.partial(pack_kernel, local_bins, slots),
        out_shape=pltpu.VMEM((2, elems, local_bins * lanes), F32),
        in_specs=[vmem] * (2 * count + 1),
        out_specs=vmem,
        compiler_params=pltpu.CompilerParams(vmem_limit_bytes=4 * MIB),
        name="pack",
    )(*near, *far, came)
    if late:
        prepare(late, 0, 34, spectra)
    for bit in middle:
        spectra = jnp.concatenate([spectra, send(spectra, tm_bit=0, rep_bit=bit)])
    own = jnp.concatenate([spectra, send(spectra, tm_bit=0, rep_bit=2)])
    other = jnp.concatenate([send(spectra, tm_bit=0, rep_bit=3), send(spectra, tm_bit=0, rep_bit=1)])
    bits = rep.bit_length() - 1
    proj = pl.pallas_call(
        functools.partial(first_kernel, snaps, bits, len(highs)),
        out_shape=pltpu.VMEM((local_bins, rows, 2 * lanes), F32),
        in_specs=[vmem] * (1 + 2 * len(highs)),
        out_specs=vmem,
        compiler_params=pltpu.CompilerParams(vmem_limit_bytes=6 * MIB),
        cost_estimate=pl.CostEstimate(flops=COST, bytes_accessed=0, transcendentals=0),
        name="first",
    )(own, *highs, *lows)
    chunk = rows // tm
    count = tm // 2
    share = pltpu.VMEM((count, chunk), F32)
    sums = [pltpu.VMEM((count, 1, chunk), F32), pltpu.VMEM((rows // 2, 2 * lanes), F32)]
    there, rights, factors = pl.pallas_call(
        functools.partial(second_kernel, elem_count, bins, snaps, bits, len(inverses)),
        out_shape=[
            share,
            pltpu.VMEM((local_bins, elem_count, 2 * lanes), BF16),
            pltpu.VMEM((local_bins, 1, 2 * lanes), F32),
        ],
        in_specs=[vmem] * (3 + 3 * len(highs)),
        out_specs=[vmem] * 3,
        scratch_shapes=sums,
        compiler_params=pltpu.CompilerParams(vmem_limit_bytes=6 * MIB),
        name="second",
    )(other, own, proj, *highs, *lows, *inverses)
    here = pl.pallas_call(
        functools.partial(third_kernel, len(inverses)),
        out_shape=share,
        in_specs=[vmem] * (3 + 3 * len(highs)),
        out_specs=vmem,
        scratch_shapes=sums,
        compiler_params=pltpu.CompilerParams(vmem_limit_bytes=6 * MIB),
        cost_estimate=pl.CostEstimate(flops=COST, bytes_accessed=0, transcendentals=0),
        name="third",
    )(rights, factors, proj, *highs, *lows, *inverses)
    total = here + send(there, tm_bit=count, rep_bit=0)
    for bit in bits_of(tm)[1:]:
        total = total[:bit] + send(total[bit:], tm_bit=bit, rep_bit=0)
    return total.reshape(chunk)


def solution(mesh):
    in_specs = (P("tm", "rep", None), P(), P(None, "tm", "rep", None))
    body = functools.partial(shards, mesh.shape["tm"], mesh.shape["rep"])
    return jax.shard_map(body, mesh=mesh, in_specs=in_specs, out_specs=P(("rep", "tm")), check_vma=False)
```
